32 devices in a mesh: section: 4 (over x, core), seq: 8 (over z, y).
Axes of the slice: x: 2, y: 2, z: 4, core: 2. Of those that a mesh axis runs over, the one named last changes fastest.
Arguments:
- activations: bfloat16 [4, 2048, 1536], P('section', 'seq'), may hold values from -6 to 6
- qkv_weight: bfloat16 [4, 1536, 4608], P('section'), may hold values from -5 to 5
- out_weight: bfloat16 [4, 1536, 1536], P('section'), may hold values from -0.15625 to 0.15625
- modulation: float32 [4, 3, 1536], P('section'), may hold values from -4 to 4
- key_blocks: int32 [16, 4], replicated, may hold values from 0 to 15, as said below
- block_counts: int32 [16], replicated, may hold values from 3 to 4, as said below
Outputs:
- advanced: bfloat16 [4, 2048, 1536], P('section', 'seq')
The draws below stay inside these ranges and needn't reach their ends.
Inputs may be any that keep to these rules, and one draw needn't show every extreme that they name: Block b belongs to group b // 2. Row b of key_blocks names first its own block, then the other blocks of its group, then 2 blocks of different groups g with 1 <= |g - b // 2| <= 2. All rows of one group name at most one block of any other group. `block_counts`: some query block uses all 4 entries.
All inputs are finite; a program needn't handle non-finite values.
Results may differ from the reference program's by a relative error of at most 0.008.
Values may be sent and summed in bfloat16 or wider, within the bound.
No kernel may reach another device: no remote copies, remote signals or barrier semaphores. Data moves between devices by JAX's collectives and lax.ppermute only.
A program may use at most 128 MiB of HBM per device.

```python
import jax
import jax.numpy as jnp
from jax import lax

D = 1536
HEADS = 12
HD = 128
BLK = 128
REMOTE = 2
SECTIONS = 4
TOKENS = 2048
BLK_DEV = 2
NBLK = 16
NSEL = 4


def draw_activations(key, part):
    base = jnp.clip(jax.random.normal(key, (SECTIONS, TOKENS, D), jnp.float32), -5.0, 5.0)
    return base.astype(jnp.bfloat16)


def draw_qkv_weight(key, part):
    inner_width = HEADS * HD
    base = jnp.clip(jax.random.normal(key, (SECTIONS, D, 3 * inner_width), jnp.float32), -4.0, 4.0) * D ** (-0.5)
    return base.astype(jnp.bfloat16)


def draw_key_blocks(key, part):
    seq_count = NBLK // BLK_DEV
    aligned = jax.random.randint(jax.random.fold_in(key, 11), (seq_count, seq_count), 0, BLK_DEV)
    block_index = jnp.arange(NBLK, dtype=jnp.int32)
    device_of = block_index // BLK_DEV
    local_of = block_index % BLK_DEV
    own_part = device_of[:, None] * BLK_DEV + (local_of[:, None] + jnp.arange(BLK_DEV, dtype=jnp.int32)[None, :]) % BLK_DEV
    candidates = jnp.array([-2, -1, 1, 2], dtype=jnp.int32)
    targets = device_of[:, None] + candidates[None, :]
    valid = (targets >= 0) & (targets < seq_count)
    ranking = jax.random.randint(jax.random.fold_in(key, 12), (NBLK, 4), 0, 1 << 20)
    ranking = ranking * 4 + jnp.arange(4, dtype=jnp.int32)[None, :] + jnp.where(valid, 0, 1 << 24)
    ordering = jnp.argsort(ranking, axis=1)[:, :REMOTE]
    offsets = jnp.take_along_axis(jnp.broadcast_to(candidates[None, :], (NBLK, 4)), ordering, axis=1)
    peers = device_of[:, None] + offsets
    far_part = peers * BLK_DEV + aligned[device_of[:, None], peers]
    return jnp.concatenate([own_part, far_part], axis=1).astype(jnp.int32)


def draw_block_counts(key, part):
    counts_drawn = jax.random.randint(jax.random.fold_in(key, 21), (NBLK,), BLK_DEV + 1, NSEL + 1)
    filled_spot = jax.random.randint(jax.random.fold_in(key, 22), (), 0, NBLK)
    return jnp.where(jnp.arange(NBLK, dtype=jnp.int32) == filled_spot, NSEL, counts_drawn).astype(jnp.int32)


def block_scale(key, shape, cuts, smallest, largest):
    level = 1.0
    for axis_at, parts in cuts:
        heights = jax.random.uniform(jax.random.fold_in(jax.random.fold_in(key, 6), axis_at), (parts,), jnp.float32, smallest / len(cuts), largest / len(cuts))
        level = level * jnp.repeat(jnp.exp(heights), shape[axis_at] // parts).reshape((-1,) + (1,) * (len(shape) - 1 - axis_at))
    return level


def noise(own_key, extent, deviation, most, shards=(), kind=jnp.bfloat16):
    drawn = jax.random.normal(own_key, extent, jnp.float32) * deviation
    if len(shards) > 0:
        drawn = block_scale(own_key, extent, shards, -0.22, 0.18) * drawn
    return jnp.clip(drawn, min=-most, max=most).astype(kind)


def setup_inputs(seed: int = 0) -> dict:
    keys = jax.random.split(jax.random.key(seed), 7)
    return {
        "activations": draw_activations(jax.random.fold_in(keys[6], 71), 0),
        "qkv_weight": draw_qkv_weight(jax.random.fold_in(keys[6], 71), 0),
        "out_weight": noise(keys[2], (SECTIONS, HEADS * HD, D), (HEADS * HD) ** -0.5, 0.15625, ((0, 4),)),
        "modulation": noise(keys[3], (SECTIONS, 3, D), 1.0, 4.0, ((0, 4),), jnp.float32),
        "key_blocks": draw_key_blocks(jax.random.fold_in(keys[6], 71), 0),
        "block_counts": draw_block_counts(jax.random.fold_in(keys[6], 71), 0),
    }


EPSILON = 1e-06

def modulated_norm(tokens_in, segment_mod):
    values = tokens_in.astype(jnp.float32)
    center = lax.optimization_barrier(jnp.mean(values, axis=-1, keepdims=True))
    spread = lax.optimization_barrier(jnp.mean(jnp.square(values - center), axis=-1, keepdims=True))
    normed = (values - center) * lax.rsqrt(spread + EPSILON)
    return (normed * (1.0 + segment_mod[1]) + segment_mod[0]).astype(jnp.bfloat16)

def segment_layer(tokens_in, weights_in, weights_out, segment_mod, key_blocks, block_counts):
    token_count = tokens_in.shape[0]
    inner_width = HEADS * HD
    block_total = token_count // BLK
    list_width = key_blocks.shape[1]
    modulated = modulated_norm(tokens_in, segment_mod)
    projected = jnp.dot(modulated, weights_in, preferred_element_type=jnp.float32).astype(jnp.bfloat16)
    query_blocks = projected[:, :inner_width].reshape(block_total, BLK, HEADS, HD)
    pair_blocks = projected[:, inner_width:].reshape(block_total, BLK, 2 * inner_width)

    def one_block(operands):
        query_block, row, count = operands
        picked = jnp.take(pair_blocks, row, axis=0).reshape(list_width * BLK, 2 * inner_width)
        key_part = picked[:, :inner_width].reshape(list_width * BLK, HEADS, HD).astype(jnp.float32)
        value_part = picked[:, inner_width:].reshape(list_width * BLK, HEADS, HD)
        scores = jnp.einsum('qhd,khd->hqk', query_block.astype(jnp.float32), key_part) * HD ** (-0.5)
        live = jnp.repeat(jnp.arange(list_width, dtype=jnp.int32) < count, BLK)
        scores = jnp.where(live[None, None, :], scores, -jnp.inf)
        row_peak = lax.optimization_barrier(jnp.max(scores, axis=-1, keepdims=True))
        exponent = jnp.exp(scores - row_peak)
        denominator = lax.optimization_barrier(jnp.sum(exponent, axis=-1, keepdims=True))
        weighted = jnp.einsum('hqk,khd->hqd', exponent.astype(jnp.bfloat16).astype(jnp.float32), value_part.astype(jnp.float32))
        return jnp.moveaxis(weighted / denominator, 0, 1)
    attended = lax.map(one_block, (query_blocks, key_blocks, block_counts))
    attended = attended.reshape(token_count, inner_width).astype(jnp.bfloat16)
    output = jnp.dot(attended, weights_out, preferred_element_type=jnp.float32)
    return (tokens_in.astype(jnp.float32) + segment_mod[2] * output).astype(jnp.bfloat16)

def reference(activations, qkv_weight, out_weight, modulation, key_blocks, block_counts):

    def advance_segment(operands):
        return segment_layer(operands[0], operands[1], operands[2], operands[3], key_blocks, block_counts)
    first_pass = lax.map(advance_segment, (activations, qkv_weight, out_weight, modulation))
    handed_over = jnp.roll(first_pass, 1, axis=0)
    return lax.map(advance_segment, (handed_over, qkv_weight, out_weight, modulation))
```

```python
import functools

import jax
import jax.numpy as jnp
from jax import lax
from jax.experimental import pallas as pl
from jax.experimental.pallas import tpu as pltpu
from jax.sharding import PartitionSpec as P

HEADS = 12
HD = 128
BLK = 128
EPSILON = 1e-06
INNER = HEADS * HD
PAIR = 2 * HD
TO_EXP2 = HD ** (-0.5) * 1.4426950408889634
MASKED = -1e30
MIB = 2**20

IN_VMEM = pl.BlockSpec(memory_space=pltpu.VMEM)
IN_SMEM = pl.BlockSpec(memory_space=pltpu.SMEM)


def beyond(me, count):
    one = me + 1 - 2 * (me % 2)
    other_one = me - 1 + 2 * (me % 2)
    two = me + 2 - 4 * ((me // 2) % 2)
    other_two = me - 2 + 4 * ((me // 2) % 2)
    return [one, other_one, two, other_two]


def partner_table(count):
    table = []
    for me in range(count):
        table.append([p if 0 <= p < count else me for p in beyond(me, count)])
    return table


def pairs_of(exchange, count):
    table = partner_table(count)
    return [(me, table[me][exchange]) for me in range(count)]


def asked_block(key_ref, target, me, blocks_here):
    width = key_ref.shape[0]
    found = jnp.int32(0)
    for row in range(blocks_here):
        for entry in range(width):
            named = key_ref[entry, target * blocks_here + row]
            mine = (named >= me * blocks_here) & (named < (me + 1) * blocks_here)
            found = jnp.where(mine, named - me * blocks_here, found)
    return found


def partners_here(me, count):
    out = []
    for p in beyond(me, count):
        out.append(jnp.where((p >= 0) & (p < count), p, me))
    return out


def pick_kernel(count, key_ref, x_ref, *rest):
    outs = rest
    me = lax.axis_index("seq")
    blocks_here = x_ref.shape[0] // BLK
    for i, target in enumerate(partners_here(me, count)):
        start = pl.multiple_of(asked_block(key_ref, target, me, blocks_here) * BLK, BLK)
        outs[i][...] = x_ref[pl.ds(start, BLK), :]


def pick_blocks(x, key_blocks, count):
    part = jax.ShapeDtypeStruct((BLK, x.shape[1]), x.dtype)
    return pl.pallas_call(
        functools.partial(pick_kernel, count),
        out_shape=[part] * 4,
        in_specs=[IN_SMEM, IN_VMEM],
        out_specs=[IN_VMEM] * 4,
        name="pick_blocks",
    )(key_blocks, x)


def norm_rows(x_ref, mod_ref, out_ref, out_row):
    rows, width = x_ref.shape
    shift = mod_ref[0]
    scale = 1.0 + mod_ref[1]
    step = 16
    for r in range(0, rows, step):
        values = x_ref[r : r + step, :].astype(jnp.float32)
        center = jnp.sum(values, axis=-1, keepdims=True) * (1.0 / width)
        values = values - center
        spread = jnp.sum(values * values, axis=-1, keepdims=True) * (1.0 / width)
        normed = values * lax.rsqrt(spread + EPSILON)
        out_ref[out_row + r : out_row + r + step, :] = (normed * scale + shift).astype(jnp.bfloat16)


def project(source, weight_ref, column, width):
    return jnp.dot(
        source, weight_ref[:, column : column + width], preferred_element_type=jnp.float32
    ).astype(jnp.bfloat16)


def own_kernel(x_ref, mod_ref, w_ref, qkv_ref, normed):
    norm_rows(x_ref, mod_ref, normed, 0)
    for c in range(0, w_ref.shape[1], 2 * PAIR):
        qkv_ref[:, c : c + 2 * PAIR] = project(normed[...], w_ref, c, 2 * PAIR)


def own_projection(x, mod, w):
    return pl.pallas_call(
        own_kernel,
        out_shape=jax.ShapeDtypeStruct((x.shape[0], w.shape[1]), jnp.bfloat16),
        in_specs=[IN_VMEM] * 3,
        out_specs=IN_VMEM,
        scratch_shapes=[pltpu.VMEM(x.shape, jnp.bfloat16)],
        compiler_params=pltpu.CompilerParams(vmem_limit_bytes=16 * MIB),
        name="own_projection",
    )(x, mod, w)


def early_kernel(a_ref, b_ref, mod_ref, w_ref, kv_ref, normed):
    norm_rows(a_ref, mod_ref, normed, 0)
    norm_rows(b_ref, mod_ref, normed, BLK)
    for c in range(0, 2 * INNER, 2 * PAIR):
        kv_ref[:, c : c + 2 * PAIR] = project(normed[...], w_ref, INNER + c, 2 * PAIR)


def early_projection(a, b, mod, w):
    return pl.pallas_call(
        early_kernel,
        out_shape=jax.ShapeDtypeStruct((2 * BLK, 2 * INNER), jnp.bfloat16),
        in_specs=[IN_VMEM] * 4,
        out_specs=IN_VMEM,
        scratch_shapes=[pltpu.VMEM((2 * BLK, a.shape[1]), jnp.bfloat16)],
        compiler_params=pltpu.CompilerParams(vmem_limit_bytes=16 * MIB),
        name="early_projection",
    )(a, b, mod, w)


def slot_of(named, me, count, blocks_here, order):
    owner = named // blocks_here
    slot = jnp.int32(0)
    for i, p in enumerate(beyond(me, count)):
        slot = jnp.where(owner == p, order.index(i), slot)
    return slot


def tail_kernel(
    count, order, with_sends, key_ref, count_ref, x_ref, qkv_ref, early_ref, c_ref, d_ref, mod_ref, w_ref, wo_ref, *rest
):
    if with_sends:
        y_ref, *sends = rest[:5]
        store, normed, attended = rest[5:]
    else:
        y_ref, sends = rest[0], []
        store, normed, attended = rest[1:]
    me = lax.axis_index("seq")
    tokens = x_ref.shape[0]
    blocks_here = tokens // BLK
    half = 2 * BLK
    norm_rows(c_ref, mod_ref, normed, 0)
    norm_rows(d_ref, mod_ref, normed, BLK)
    remote = key_ref.shape[0] - blocks_here
    starts, alive = [], []
    for i in range(blocks_here):
        row = me * blocks_here + i
        listed = count_ref[row]
        starts.append(
            [
                pl.multiple_of(slot_of(key_ref[blocks_here + j, row], me, count, blocks_here, order) * BLK, BLK)
                for j in range(remote)
            ]
        )
        alive.append([blocks_here + j < listed for j in range(remote)])
    for pair in range(HEADS // 2):
        at = pair * PAIR
        store[0:half, at : at + PAIR] = early_ref[:, at : at + PAIR]
        store[0:half, INNER + at : INNER + at + PAIR] = early_ref[:, INNER + at : INNER + at + PAIR]
        store[half : 2 * half, at : at + PAIR] = project(normed[...], w_ref, INNER + at, PAIR)
        store[half : 2 * half, INNER + at : INNER + at + PAIR] = project(normed[...], w_ref, 2 * INNER + at, PAIR)
        for h in (2 * pair, 2 * pair + 1):
            col = h * HD
            q = qkv_ref[:, col : col + HD]
            k_own = qkv_ref[:, INNER + col : INNER + col + HD]
            v_own = qkv_ref[:, 2 * INNER + col : 2 * INNER + col + HD]
            s_own_all = lax.dot_general(
                q, k_own, (((1,), (1,)), ((), ())), preferred_element_type=jnp.float32
            )
            for i in range(blocks_here):
                rows = slice(i * BLK, (i + 1) * BLK)
                s_own = s_own_all[rows]
                k_far = jnp.concatenate(
                    [store[pl.ds(s, BLK), col : col + HD] for s in starts[i]], axis=0
                )
                v_far = jnp.concatenate(
                    [store[pl.ds(s, BLK), INNER + col : INNER + col + HD] for s in starts[i]], axis=0
                )
                s_far = lax.dot_general(
                    q[rows], k_far, (((1,), (1,)), ((), ())), preferred_element_type=jnp.float32
                )
                far = [
                    jnp.where(alive[i][j], s_far[:, j * BLK : (j + 1) * BLK], MASKED) for j in range(remote)
                ]
                s_all = jnp.concatenate([s_own] + far, axis=1)
                peak = jnp.max(s_all, axis=-1, keepdims=True)
                p = jnp.exp2((s_all - peak) * TO_EXP2)
                total = jnp.sum(p, axis=-1, keepdims=True)
                weighted = jnp.dot(
                    p.astype(jnp.bfloat16),
                    jnp.concatenate([v_own, v_far], axis=0),
                    preferred_element_type=jnp.float32,
                )
                attended[rows, col : col + HD] = (weighted / total).astype(jnp.bfloat16)
    for c in range(0, wo_ref.shape[1], 2 * PAIR):
        cols = slice(c, c + 2 * PAIR)
        out = jnp.dot(attended[...], wo_ref[:, cols], preferred_element_type=jnp.float32)
        y_ref[:, cols] = (x_ref[:, cols].astype(jnp.float32) + mod_ref[2, :, cols] * out).astype(jnp.bfloat16)
    for send, target in zip(sends, partners_here(me, count)):
        start = pl.multiple_of(asked_block(key_ref, target, me, blocks_here) * BLK, BLK)
        send[...] = y_ref[pl.ds(start, BLK), :]


def tail(x, qkv, early, late, mod, w, wo, key_blocks, block_counts, count, order, with_sends):
    part = jax.ShapeDtypeStruct((BLK, x.shape[1]), x.dtype)
    whole = jax.ShapeDtypeStruct(x.shape, x.dtype)
    return pl.pallas_call(
        functools.partial(tail_kernel, count, order, with_sends),
        out_shape=[whole] + [part] * (4 if with_sends else 0),
        in_specs=[IN_SMEM] * 2 + [IN_VMEM] * 8,
        out_specs=[IN_VMEM] * (5 if with_sends else 1),
        scratch_shapes=[
            pltpu.VMEM((4 * BLK, 2 * INNER), jnp.bfloat16),
            pltpu.VMEM((2 * BLK, x.shape[1]), jnp.bfloat16),
            pltpu.VMEM((x.shape[0], INNER), jnp.bfloat16),
        ],
        compiler_params=pltpu.CompilerParams(vmem_limit_bytes=16 * MIB),
        name="tail",
    )(key_blocks, block_counts, x, qkv, early, *late, mod, w, wo)


def on_device(activations, qkv_weight, out_weight, modulation, key_blocks, block_counts):
    count = lax.axis_size("seq")
    sections = lax.axis_size("section")
    x, w, wo = activations[0], qkv_weight[0], out_weight[0]
    mod = modulation.reshape(modulation.shape[1], 1, modulation.shape[2])
    key_blocks = key_blocks.T
    order = [1, 0, 2, 3]

    sends = pick_blocks(x, key_blocks, count)
    got = [lax.ppermute(sends[i], "seq", pairs_of(i, count)) for i in order]
    qkv = own_projection(x, mod, w)
    early = early_projection(got[0], got[1], mod, w)
    y, *sends = tail(
        x, qkv, early, got[2:], mod, w, wo, key_blocks, block_counts, count, order, True
    )

    x2 = lax.ppermute(y, "section", [(s, (s + 1) % sections) for s in range(sections)])
    got = []
    for i in order:
        moved = [
            (s * count + a, (s + 1) % sections * count + b)
            for s in range(sections)
            for a, b in pairs_of(i, count)
        ]
        got.append(lax.ppermute(sends[i], ("section", "seq"), moved))
    qkv = own_projection(x2, mod, w)
    early = early_projection(got[0], got[1], mod, w)
    (out,) = tail(
        x2, qkv, early, got[2:], mod, w, wo, key_blocks, block_counts, count, order, False
    )
    return out[None]


def solution(mesh):
    return jax.shard_map(
        on_device,
        mesh=mesh,
        in_specs=(
            P("section", "seq", None),
            P("section", None, None),
            P("section", None, None),
            P("section", None, None),
            P(),
            P(),
        ),
        out_specs=P("section", "seq", None),
        check_vma=False,
    )
```

```python
import functools

import jax
import jax.numpy as jnp
from jax import lax
from jax.experimental import pallas as pl
from jax.experimental.pallas import tpu as pltpu
from jax.sharding import PartitionSpec as P

HEADS = 12
HD = 128
BLK = 128
EPSILON = 1e-06
INNER = HEADS * HD
PAIR = 2 * HD
TO_EXP2 = HD ** (-0.5) * 1.4426950408889634
MASKED = -1e30
EARLY = (1, 0, 2, 3)
LATE = ()
FIRST_TAKEN = (1,)
LIMIT = 16 * 2**20
FIRST_LIMIT = 30 * 2**20

IN_VMEM = pl.BlockSpec(memory_space=pltpu.VMEM)
IN_SMEM = pl.BlockSpec(memory_space=pltpu.SMEM)
IN_HBM = pl.BlockSpec(memory_space=pltpu.HBM)


def beyond(me, count):
    one = me + 1 - 2 * (me % 2)
    other_one = me - 1 + 2 * (me % 2)
    two = me + 2 - 4 * ((me // 2) % 2)
    other_two = me - 2 + 4 * ((me // 2) % 2)
    return [one, other_one, two, other_two]


def partner_table(count):
    table = []
    for me in range(count):
        table.append([p if 0 <= p < count else me for p in beyond(me, count)])
    return table


def pairs_of(exchange, count):
    table = partner_table(count)
    return [(me, table[me][exchange]) for me in range(count)]


def asked_block(key_ref, target, me, blocks_here):
    width = key_ref.shape[0]
    found = jnp.int32(0)
    for row in range(blocks_here):
        for entry in range(width):
            named = key_ref[entry, target * blocks_here + row]
            mine = (named >= me * blocks_here) & (named < (me + 1) * blocks_here)
            found = jnp.where(mine, named - me * blocks_here, found)
    return found


def partners_here(me, count):
    out = []
    for p in beyond(me, count):
        out.append(jnp.where((p >= 0) & (p < count), p, me))
    return out


def pick_first_kernel(count, exchanges, key_ref, x_in, mod_in, x_ref, mod_ref, *sends):
    send_asked(count, exchanges, key_ref, x_in, sends)
    x_ref[...] = x_in[...]
    mod_ref[...] = mod_in[...]


def pick_first(x, mod, key_blocks, count, exchanges):
    part = jax.ShapeDtypeStruct((BLK, x.shape[1]), x.dtype)
    return pl.pallas_call(
        functools.partial(pick_first_kernel, count, exchanges),
        out_shape=[jax.ShapeDtypeStruct(a.shape, a.dtype) for a in (x, mod)] + [part] * len(exchanges),
        in_specs=[IN_SMEM, IN_VMEM, IN_VMEM],
        out_specs=[IN_VMEM] * (2 + len(exchanges)),
        compiler_params=pltpu.CompilerParams(vmem_limit_bytes=LIMIT),
        name="pick_first",
    )(key_blocks, x, mod)


def pick_kernel(count, exchanges, key_ref, x_ref, *sends):
    send_asked(count, exchanges, key_ref, x_ref, sends)


def pick_blocks(x, key_blocks, count, exchanges):
    part = jax.ShapeDtypeStruct((BLK, x.shape[1]), x.dtype)
    return pl.pallas_call(
        functools.partial(pick_kernel, count, exchanges),
        out_shape=[part] * len(exchanges),
        in_specs=[IN_SMEM, IN_VMEM],
        out_specs=[IN_VMEM] * len(exchanges),
        compiler_params=pltpu.CompilerParams(vmem_limit_bytes=LIMIT),
        name="pick_blocks",
    )(key_blocks, x)


def send_asked(count, exchanges, key_ref, y_ref, sends):
    me = lax.axis_index("seq")
    blocks_here = y_ref.shape[0] // BLK
    for exchange, send in zip(exchanges, sends):
        target = partners_here(me, count)[exchange]
        start = pl.multiple_of(asked_block(key_ref, target, me, blocks_here) * BLK, BLK)
        send[...] = y_ref[pl.ds(start, BLK), :]


def norm_rows(x_ref, mod_ref, out_ref, out_row):
    rows, width = x_ref.shape
    shift = mod_ref[0]
    scale = 1.0 + mod_ref[1]
    step = 16
    for r in range(0, rows, step):
        values = x_ref[r : r + step, :].astype(jnp.float32)
        center = jnp.sum(values, axis=-1, keepdims=True) * (1.0 / width)
        values = values - center
        spread = jnp.sum(values * values, axis=-1, keepdims=True) * (1.0 / width)
        normed = values * lax.rsqrt(spread + EPSILON)
        out_ref[out_row + r : out_row + r + step, :] = (normed * scale + shift).astype(jnp.bfloat16)


def project(source, weight_ref, column, width):
    return jnp.dot(
        source, weight_ref[:, column : column + width], preferred_element_type=jnp.float32
    ).astype(jnp.bfloat16)


def scores_of(q, k):
    return lax.dot_general(q, k, (((1,), (1,)), ((), ())), preferred_element_type=jnp.float32)


def with_ones(v):
    return jnp.concatenate([v, jnp.ones(v.shape, v.dtype)], axis=1)


def own_heads(normed, w_ref, q_ref, kv, peak_ref, total_ref, acc_ref, before):
    wide = 4 * HD
    for n, at in enumerate(range(0, INNER, wide)):
        cols = slice(at, at + wide)
        before(3 * n)
        q_ref[:, cols] = project(normed[...], w_ref, at, wide)
        before(3 * n + 1)
        kv[:, cols] = project(normed[...], w_ref, INNER + at, wide)
        before(3 * n + 2)
        kv[:, INNER + at : INNER + at + wide] = project(normed[...], w_ref, 2 * INNER + at, wide)
        for h in range(at, at + wide, HD):
            here = slice(h, h + HD)
            s = scores_of(q_ref[:, here], kv[:, here])
            peak = jnp.max(s, axis=-1, keepdims=True)
            p = jnp.exp2((s - peak) * TO_EXP2).astype(jnp.bfloat16)
            both = jnp.dot(p, with_ones(kv[:, INNER + h : INNER + h + HD]), preferred_element_type=jnp.float32)
            peak_ref[:, here] = jnp.broadcast_to(peak, (s.shape[0], HD))
            total_ref[:, here] = both[:, HD:]
            acc_ref[:, here] = both[:, :HD]


def first_kernel(
    count, key_ref, x_ref, mod_ref, w_hbm, q_ref, peak_ref, total_ref, acc_ref, w_ref, *rest
):
    sends, (normed, kv, sems) = rest[:-3], rest[-3:]
    wide = 4 * HD
    copies = []
    for at in range(0, INNER, wide):
        for c in (at, INNER + at, 2 * INNER + at):
            n = len(copies)
            cols = slice(c, c + wide)
            copies.append(pltpu.make_async_copy(w_hbm.at[:, cols], w_ref.at[:, cols], sems.at[n]))
            copies[n].start()
    send_asked(count, LATE, key_ref, x_ref, sends)
    norm_rows(x_ref, mod_ref, normed, 0)
    own_heads(normed, w_ref, q_ref, kv, peak_ref, total_ref, acc_ref, lambda n: copies[n].wait())


def own_scratch(tokens, width):
    return [pltpu.VMEM((tokens, width), jnp.bfloat16), pltpu.VMEM((tokens, 2 * INNER), jnp.bfloat16)]


def first_part(x, mod, w, key_blocks, count):
    tokens, width = x.shape
    state = jax.ShapeDtypeStruct((tokens, INNER), jnp.float32)
    held = [jax.ShapeDtypeStruct(shape, jnp.bfloat16) for shape in [(tokens, INNER), w.shape] + [(BLK, width)] * len(LATE)]
    return pl.pallas_call(
        functools.partial(first_kernel, count),
        out_shape=held[:1] + [state] * 3 + held[1:],
        in_specs=[IN_SMEM, IN_VMEM, IN_VMEM, IN_HBM],
        out_specs=[IN_VMEM] * (5 + len(LATE)),
        scratch_shapes=own_scratch(tokens, width) + [pltpu.SemaphoreType.DMA((w.shape[1] // (2 * PAIR),))],
        compiler_params=pltpu.CompilerParams(vmem_limit_bytes=FIRST_LIMIT),
        name="first_part",
    )(key_blocks, x, mod, w)


def second_kernel(count, key_ref, x_ref, mod_ref, w_ref, q_ref, peak_ref, total_ref, acc_ref, *rest):
    sends, (normed, kv) = rest[:-2], rest[-2:]
    send_asked(count, LATE, key_ref, x_ref, sends)
    norm_rows(x_ref, mod_ref, normed, 0)
    own_heads(normed, w_ref, q_ref, kv, peak_ref, total_ref, acc_ref, lambda n: None)


def second_part(x, mod, w, key_blocks, count):
    tokens, width = x.shape
    state = jax.ShapeDtypeStruct((tokens, INNER), jnp.float32)
    return pl.pallas_call(
        functools.partial(second_kernel, count),
        out_shape=[jax.ShapeDtypeStruct((tokens, INNER), jnp.bfloat16)]
        + [state] * 3
        + [jax.ShapeDtypeStruct((BLK, width), x.dtype)] * len(LATE),
        in_specs=[IN_SMEM] + [IN_VMEM] * 3,
        out_specs=[IN_VMEM] * (4 + len(LATE)),
        scratch_shapes=own_scratch(tokens, width),
        compiler_params=pltpu.CompilerParams(vmem_limit_bytes=LIMIT),
        name="second_part",
    )(key_blocks, x, mod, w)


def uses(key_ref, count_ref, me, owner, blocks_here):
    used = jnp.bool_(False)
    for i in range(blocks_here):
        row = me * blocks_here + i
        for j in range(blocks_here, key_ref.shape[0]):
            used = used | ((key_ref[j, row] // blocks_here == owner) & (j < count_ref[row]))
    return used & (owner != me)


def project_block(block_ref, mod_ref, w_ref, normed, row, kv_ref):
    rows = slice(row, row + BLK)
    norm_rows(block_ref, mod_ref, normed, row)
    for c in range(0, 2 * INNER, 2 * PAIR):
        kv_ref[rows, c : c + 2 * PAIR] = project(normed[rows, :], w_ref, INNER + c, 2 * PAIR)


def arrived_kernel(count, exchanges, blocks_here, key_ref, count_ref, *rest):
    blocks, (mod_ref, w_ref, kv_ref, normed) = rest[: len(exchanges)], rest[len(exchanges) :]
    me = lax.axis_index("seq")
    partners = partners_here(me, count)
    for n, exchange in enumerate(exchanges):

        @pl.when(uses(key_ref, count_ref, me, partners[exchange], blocks_here))
        def _():
            project_block(blocks[n], mod_ref, w_ref, normed, n * BLK, kv_ref)


def arrived_part(count, exchanges, blocks_here, key_blocks, block_counts, blocks, mod, w):
    rows = len(exchanges) * BLK
    return pl.pallas_call(
        functools.partial(arrived_kernel, count, exchanges, blocks_here),
        out_shape=jax.ShapeDtypeStruct((rows, 2 * INNER), jnp.bfloat16),
        in_specs=[IN_SMEM] * 2 + [IN_VMEM] * (len(blocks) + 2),
        out_specs=IN_VMEM,
        scratch_shapes=[pltpu.VMEM((rows, w.shape[0]), jnp.bfloat16)],
        compiler_params=pltpu.CompilerParams(vmem_limit_bytes=LIMIT),
        name="arrived_part",
    )(key_blocks, block_counts, *blocks, mod, w)


def last_kernel(
    count, key_ref, count_ref, two_ref, other_one_ref, block_ref, q_ref, peak_ref, total_ref, acc_ref, x_ref, mod_ref,
    w_ref, wo_ref, y_ref, normed, one_ref, attended,
):
    me = lax.axis_index("seq")
    blocks_here = x_ref.shape[0] // BLK
    remote = key_ref.shape[0] - blocks_here
    partners = partners_here(me, count)

    @pl.when(uses(key_ref, count_ref, me, partners[0], blocks_here))
    def _():
        project_block(block_ref, mod_ref, w_ref, normed, 0, one_ref)

    chosen, bias = [], []
    for i in range(blocks_here):
        row = me * blocks_here + i
        owners = [key_ref[blocks_here + j, row] // blocks_here for j in range(remote)]
        live = [blocks_here + j < count_ref[row] for j in range(remote)]
        owners = [jnp.where(live[j], owners[j], owners[0]) for j in range(remote)]
        bias.append([jnp.where(live[j], 0.0, MASKED) for j in range(remote)])
        chosen.append(
            [
                (
                    pl.multiple_of(jnp.where(owner == partners[3], BLK, 0), BLK),
                    owner == partners[1],
                    owner == partners[0],
                )
                for owner in owners
            ]
        )

    def block_of(i, cols):
        parts = []
        for start, is_other_one, is_one in chosen[i]:
            part = two_ref[pl.ds(start, BLK), cols]
            part = jnp.where(is_other_one, other_one_ref[:, cols], part)
            parts.append(jnp.where(is_one, one_ref[:, cols], part))
        return jnp.concatenate(parts, axis=0)

    for at in range(0, INNER, HD):
        here = slice(at, at + HD)
        for i in range(blocks_here):
            rows = slice(i * BLK, (i + 1) * BLK)
            s = scores_of(q_ref[rows, here], block_of(i, here))
            s = [s[:, j * BLK : (j + 1) * BLK] + bias[i][j] for j in range(remote)]
            old_peak = peak_ref[rows, here]
            peak = old_peak
            for part in s:
                peak = jnp.maximum(peak, jnp.max(part, axis=-1, keepdims=True))
            p = jnp.concatenate([jnp.exp2((part - peak) * TO_EXP2).astype(jnp.bfloat16) for part in s], axis=1)
            v = with_ones(block_of(i, slice(INNER + at, INNER + at + HD)))
            both = jnp.dot(p, v, preferred_element_type=jnp.float32)
            keep = jnp.exp2((old_peak - peak) * TO_EXP2)
            total = total_ref[rows, here] * keep + both[:, HD:]
            acc = acc_ref[rows, here] * keep + both[:, :HD]
            attended[rows, here] = (acc / total).astype(jnp.bfloat16)
    for c in range(0, wo_ref.shape[1], 2 * PAIR):
        cols = slice(c, c + 2 * PAIR)
        out = jnp.dot(attended[...], wo_ref[:, cols], preferred_element_type=jnp.float32)
        y_ref[:, cols] = (x_ref[:, cols].astype(jnp.float32) + mod_ref[2, :, cols] * out).astype(jnp.bfloat16)


def last_part(count, key_blocks, block_counts, two, other_one, block, q, state, x, mod, w, wo):
    return pl.pallas_call(
        functools.partial(last_kernel, count),
        out_shape=jax.ShapeDtypeStruct(x.shape, x.dtype),
        in_specs=[IN_SMEM] * 2 + [IN_VMEM] * 11,
        out_specs=IN_VMEM,
        scratch_shapes=[
            pltpu.VMEM((BLK, w.shape[0]), jnp.bfloat16),
            pltpu.VMEM((BLK, 2 * INNER), jnp.bfloat16),
            pltpu.VMEM((x.shape[0], INNER), jnp.bfloat16),
        ],
        compiler_params=pltpu.CompilerParams(vmem_limit_bytes=LIMIT),
        name="last_part",
    )(key_blocks, block_counts, two, other_one, block, q, *state, x, mod, w, wo)


def rest_of_layer(x, q, state, got, mod, w, wo, key_blocks, block_counts, count):
    lists_of = (key_blocks, block_counts)
    blocks_here = x.shape[0] // BLK
    other_one = arrived_part(count, (1,), blocks_here, *lists_of, [got[1]], mod, w)
    two = arrived_part(count, (2, 3), blocks_here, *lists_of, [got[2], got[3]], mod, w)
    return last_part(count, *lists_of, two, other_one, got[0], q, state, x, mod, w, wo)


def exchanged(sends, exchanges, count):
    return {i: lax.ppermute(send, "seq", pairs_of(i, count)) for i, send in zip(exchanges, sends)}


def on_device(activations, qkv_weight, out_weight, modulation, key_blocks, block_counts):
    count = lax.axis_size("seq")
    sections = lax.axis_size("section")
    x, w, wo = activations[0], qkv_weight[0], out_weight[0]
    mod = modulation.reshape(modulation.shape[1], 1, modulation.shape[2])
    key_blocks = key_blocks.T

    x, mod, *sends = pick_first(x, mod, key_blocks, count, EARLY)
    got = exchanged(sends, EARLY, count)
    q, peak, total, acc, w, *sends = first_part(x, mod, w, key_blocks, count)
    got.update(exchanged(sends, LATE, count))
    y = rest_of_layer(x, q, (peak, total, acc), got, mod, w, wo, key_blocks, block_counts, count)

    x = lax.ppermute(y, "section", [(s, (s + 1) % sections) for s in range(sections)])
    sends = pick_blocks(x, key_blocks, count, EARLY)
    got = exchanged(sends, EARLY, count)
    q, peak, total, acc, *sends = second_part(x, mod, w, key_blocks, count)
    got.update(exchanged(sends, LATE, count))
    out = rest_of_layer(x, q, (peak, total, acc), got, mod, w, wo, key_blocks, block_counts, count)
    return out[None]


def solution(mesh):
    return jax.shard_map(
        on_device,
        mesh=mesh,
        in_specs=(
            P("section", "seq", None),
            P("section", None, None),
            P("section", None, None),
            P("section", None, None),
            P(),
            P(),
        ),
        out_specs=P("section", "seq", None),
        check_vma=False,
    )
```

```python
import functools

import jax
import jax.numpy as jnp
from jax import lax
from jax.experimental import pallas as pl
from jax.experimental.pallas import tpu as pltpu
from jax.sharding import PartitionSpec as P

HEADS = 12
HD = 128
BLK = 128
EPSILON = 1e-06
INNER = HEADS * HD
PAIR = 2 * HD
TO_EXP2 = HD ** (-0.5) * 1.4426950408889634
MASKED = -1e30
EARLY = 1
LATE = (0, 2, 3)
PIECES = 2
DIRECT = (1,)
LIMIT = 16 * 2**20
FIRST_LIMIT = 30 * 2**20

IN_VMEM = pl.BlockSpec(memory_space=pltpu.VMEM)
IN_SMEM = pl.BlockSpec(memory_space=pltpu.SMEM)
IN_HBM = pl.BlockSpec(memory_space=pltpu.HBM)


def beyond(me, count):
    one = me + 1 - 2 * (me % 2)
    other_one = me - 1 + 2 * (me % 2)
    two = me + 2 - 4 * ((me // 2) % 2)
    other_two = me - 2 + 4 * ((me // 2) % 2)
    return [one, other_one, two, other_two]


def partner_table(count):
    table = []
    for me in range(count):
        table.append([p if 0 <= p < count else me for p in beyond(me, count)])
    return table


def pairs_of(exchange, count):
    table = partner_table(count)
    return [(me, table[me][exchange]) for me in range(count)]


def asked_block(key_ref, target, me, blocks_here):
    width = key_ref.shape[0]
    found = jnp.int32(0)
    for row in range(blocks_here):
        for entry in range(width):
            named = key_ref[entry, target * blocks_here + row]
            mine = (named >= me * blocks_here) & (named < (me + 1) * blocks_here)
            found = jnp.where(mine, named - me * blocks_here, found)
    return found


def partners_here(me, count):
    out = []
    for p in beyond(me, count):
        out.append(jnp.where((p >= 0) & (p < count), p, me))
    return out


def pick_kernel(count, exchanges, parts, key_ref, *refs):
    send_asked(count, exchanges, key_ref, refs[:parts], refs[parts:])


def pick_blocks(parts, key_blocks, count, exchanges, params=None):
    width = parts[0].shape[1]
    return pl.pallas_call(
        functools.partial(pick_kernel, count, exchanges, len(parts)),
        out_shape=[jax.ShapeDtypeStruct((BLK, width), parts[0].dtype)] * len(exchanges),
        in_specs=[IN_SMEM] + [IN_VMEM] * len(parts),
        out_specs=[IN_VMEM] * len(exchanges),
        compiler_params=params,
        name="pick_blocks",
    )(key_blocks, *parts)


def send_asked(count, exchanges, key_ref, parts, sends):
    me = lax.axis_index("seq")
    rows = parts[0].shape[0]
    blocks_here = len(parts) * rows // BLK
    for exchange, send in zip(exchanges, sends):
        block = asked_block(key_ref, partners_here(me, count)[exchange], me, blocks_here)
        if len(parts) == 1:
            send[...] = parts[0][pl.ds(pl.multiple_of(block * BLK, BLK), BLK), :]
        else:
            each = BLK // rows
            for n in range(blocks_here):

                @pl.when(block == n)
                def _():
                    for m in range(each):
                        send[m * rows : (m + 1) * rows, :] = parts[n * each + m][...]


def norm_rows(x_ref, mod_ref, out_ref, out_row):
    rows, width = x_ref.shape
    shift = mod_ref[0]
    scale = 1.0 + mod_ref[1]
    step = 16
    for r in range(0, rows, step):
        values = x_ref[r : r + step, :].astype(jnp.float32)
        center = jnp.sum(values, axis=-1, keepdims=True) * (1.0 / width)
        values = values - center
        spread = jnp.sum(values * values, axis=-1, keepdims=True) * (1.0 / width)
        normed = values * lax.rsqrt(spread + EPSILON)
        out_ref[out_row + r : out_row + r + step, :] = (normed * scale + shift).astype(jnp.bfloat16)


def project(source, weight_ref, column, width):
    return jnp.dot(
        source, weight_ref[:, column : column + width], preferred_element_type=jnp.float32
    ).astype(jnp.bfloat16)


def scores_of(q, k):
    return lax.dot_general(q, k, (((1,), (1,)), ((), ())), preferred_element_type=jnp.float32)


def with_ones(v):
    return jnp.concatenate([v, jnp.ones(v.shape, v.dtype)], axis=1)


def own_columns():
    wide = 4 * HD
    for at in range(0, INNER, wide):
        yield at, wide


def own_heads(normed, w_ref, q_ref, kv, peak_ref, total_ref, acc_ref, row, before):
    rows = slice(row, q_ref.shape[0])
    for n, (at, wide) in enumerate(own_columns()):
        cols = slice(at, at + wide)
        before(3 * n)
        q_ref[rows, cols] = project(normed[...], w_ref, at, wide)
        before(3 * n + 1)
        kv[rows, cols] = project(normed[...], w_ref, INNER + at, wide)
        before(3 * n + 2)
        kv[rows, INNER + at : INNER + at + wide] = project(normed[...], w_ref, 2 * INNER + at, wide)
        for h in range(at, at + wide, HD):
            here = slice(h, h + HD)
            s = scores_of(q_ref[:, here], kv[:, here])
            peak = jnp.max(s, axis=-1, keepdims=True)
            p = jnp.exp2((s - peak) * TO_EXP2).astype(jnp.bfloat16)
            both = jnp.dot(p, with_ones(kv[:, INNER + h : INNER + h + HD]), preferred_element_type=jnp.float32)
            peak_ref[:, here] = jnp.broadcast_to(peak, (s.shape[0], HD))
            total_ref[:, here] = both[:, HD:]
            acc_ref[:, here] = both[:, :HD]


def first_kernel(
    x_ref, mod_ref, w_hbm, q_ref, peak_ref, total_ref, acc_ref, w_ref, normed, kv, sems
):
    wide = 4 * HD
    copies = []
    for at in range(0, INNER, wide):
        for c in (at, INNER + at, 2 * INNER + at):
            n = len(copies)
            cols = slice(c, c + wide)
            copies.append(pltpu.make_async_copy(w_hbm.at[:, cols], w_ref.at[:, cols], sems.at[n]))
            copies[n].start()
    norm_rows(x_ref, mod_ref, normed, 0)
    own_heads(normed, w_ref, q_ref, kv, peak_ref, total_ref, acc_ref, 0, lambda n: copies[n].wait())


def own_scratch(tokens, width):
    return [pltpu.VMEM((tokens, width), jnp.bfloat16), pltpu.VMEM((tokens, 2 * INNER), jnp.bfloat16)]


def first_part(x, mod, w):
    tokens, width = x.shape
    state = jax.ShapeDtypeStruct((tokens, INNER), jnp.float32)
    held = [jax.ShapeDtypeStruct(shape, jnp.bfloat16) for shape in [(tokens, INNER), w.shape]]
    return pl.pallas_call(
        first_kernel,
        out_shape=held[:1] + [state] * 3 + held[1:],
        in_specs=[IN_VMEM, IN_VMEM, IN_HBM],
        out_specs=[IN_VMEM] * 5,
        scratch_shapes=own_scratch(tokens, width) + [pltpu.SemaphoreType.DMA((w.shape[1] // (2 * PAIR),))],
        compiler_params=pltpu.CompilerParams(vmem_limit_bytes=FIRST_LIMIT),
        name="first_part",
    )(x, mod, w)


def half_kernel(x_ref, mod_ref, w_ref, qkv_ref, normed):
    norm_rows(x_ref, mod_ref, normed, 0)
    for c in range(0, 3 * INNER, 4 * HD):
        qkv_ref[:, c : c + 4 * HD] = project(normed[...], w_ref, c, 4 * HD)


def half_part(x, mod, w):
    rows, width = x.shape
    return pl.pallas_call(
        half_kernel,
        out_shape=jax.ShapeDtypeStruct((rows, w.shape[1]), jnp.bfloat16),
        in_specs=[IN_VMEM] * 3,
        out_specs=IN_VMEM,
        scratch_shapes=[pltpu.VMEM((rows, width), jnp.bfloat16)],
        compiler_params=pltpu.CompilerParams(vmem_limit_bytes=LIMIT),
        name="half_part",
    )(x, mod, w)


def second_kernel(a_ref, b_ref, qkv_ref, mod_ref, w_ref, x_ref, q_ref, peak_ref, total_ref, acc_ref, normed, kv):
    rows = a_ref.shape[0]
    x_ref[:rows, :] = a_ref[...]
    x_ref[rows:, :] = b_ref[...]
    q_ref[:rows, :] = qkv_ref[:, :INNER]
    kv[:rows, :] = qkv_ref[:, INNER:]
    norm_rows(b_ref, mod_ref, normed, 0)
    own_heads(normed, w_ref, q_ref, kv, peak_ref, total_ref, acc_ref, rows, lambda n: None)


def second_part(a, b, qkv, mod, w):
    tokens, width = a.shape[0] + b.shape[0], a.shape[1]
    state = jax.ShapeDtypeStruct((tokens, INNER), jnp.float32)
    half = [jax.ShapeDtypeStruct(shape, jnp.bfloat16) for shape in ((tokens, width), (tokens, INNER))]
    return pl.pallas_call(
        second_kernel,
        out_shape=half + [state] * 3,
        in_specs=[IN_VMEM] * 5,
        out_specs=[IN_VMEM] * 5,
        scratch_shapes=[
            pltpu.VMEM(b.shape, jnp.bfloat16),
            pltpu.VMEM((tokens, 2 * INNER), jnp.bfloat16),
        ],
        compiler_params=pltpu.CompilerParams(vmem_limit_bytes=LIMIT),
        name="second_part",
    )(a, b, qkv, mod, w)


def uses(key_ref, count_ref, me, owner, blocks_here):
    used = jnp.bool_(False)
    for i in range(blocks_here):
        row = me * blocks_here + i
        for j in range(blocks_here, key_ref.shape[0]):
            used = used | ((key_ref[j, row] // blocks_here == owner) & (j < count_ref[row]))
    return used & (owner != me)


def project_block(block_ref, mod_ref, w_ref, normed, row, kv_ref):
    rows = slice(row, row + BLK)
    norm_rows(block_ref, mod_ref, normed, row)
    for c in range(0, 2 * INNER, 2 * PAIR):
        kv_ref[rows, c : c + 2 * PAIR] = project(normed[rows, :], w_ref, INNER + c, 2 * PAIR)


def arrived_kernel(count, exchanges, blocks_here, key_ref, count_ref, *rest):
    blocks, (mod_ref, w_ref, kv_ref, normed) = rest[: len(exchanges)], rest[len(exchanges) :]
    me = lax.axis_index("seq")
    partners = partners_here(me, count)
    for n, exchange in enumerate(exchanges):

        @pl.when(uses(key_ref, count_ref, me, partners[exchange], blocks_here))
        def _():
            project_block(blocks[n], mod_ref, w_ref, normed, n * BLK, kv_ref)


def arrived_part(count, exchanges, blocks_here, key_blocks, block_counts, blocks, mod, w):
    rows = len(exchanges) * BLK
    return pl.pallas_call(
        functools.partial(arrived_kernel, count, exchanges, blocks_here),
        out_shape=jax.ShapeDtypeStruct((rows, 2 * INNER), jnp.bfloat16),
        in_specs=[IN_SMEM] * 2 + [IN_VMEM] * (len(blocks) + 2),
        out_specs=IN_VMEM,
        scratch_shapes=[pltpu.VMEM((rows, w.shape[0]), jnp.bfloat16)],
        compiler_params=pltpu.CompilerParams(vmem_limit_bytes=LIMIT),
        name="arrived_part",
    )(key_blocks, block_counts, *blocks, mod, w)


def last_kernel(count, early, late, asked, pieces, key_ref, count_ref, *rest):
    early_refs, rest = rest[: len(early)], rest[len(early) :]
    blocks, rest = rest[: len(late)], rest[len(late) :]
    q_ref, peak_ref, total_ref, acc_ref, x_ref, mod_ref, w_ref, wo_ref, *rest = rest
    ys, sends, (normed, kv, attended) = rest[:pieces], rest[pieces:-3], rest[-3:]
    me = lax.axis_index("seq")
    tokens = x_ref.shape[0]
    blocks_here = tokens // BLK
    remote = key_ref.shape[0] - blocks_here
    partners = partners_here(me, count)
    slots = early + late
    for n, exchange in enumerate(slots):

        @pl.when(uses(key_ref, count_ref, me, partners[exchange], blocks_here))
        def _():
            if n < len(early):
                kv[n * BLK : (n + 1) * BLK, :] = early_refs[n][...]
            else:
                project_block(blocks[n - len(early)], mod_ref, w_ref, normed, n * BLK, kv)

    starts, bias = [], []
    for i in range(blocks_here):
        row = me * blocks_here + i
        starts.append([])
        bias.append([])
        for j in range(remote):
            live = blocks_here + j < count_ref[row]
            bias[i].append(jnp.where(live, 0.0, MASKED))
            owner = key_ref[blocks_here + j, row] // blocks_here
            owner = jnp.where(live, owner, key_ref[blocks_here, row] // blocks_here)
            start = jnp.int32(0)
            for n, exchange in enumerate(slots):
                start = jnp.where(owner == partners[exchange], n * BLK, start)
            starts[i].append(pl.multiple_of(start, BLK))

    def listed(i, cols):
        return jnp.concatenate([kv[pl.ds(start, BLK), cols] for start in starts[i]], axis=0)

    for at in range(0, INNER, HD):
        here = slice(at, at + HD)
        for i in range(blocks_here):
            rows = slice(i * BLK, (i + 1) * BLK)
            s = scores_of(q_ref[rows, here], listed(i, here))
            s = [s[:, j * BLK : (j + 1) * BLK] + bias[i][j] for j in range(remote)]
            old_peak = peak_ref[rows, here]
            peak = old_peak
            for part in s:
                peak = jnp.maximum(peak, jnp.max(part, axis=-1, keepdims=True))
            p = jnp.concatenate([jnp.exp2((part - peak) * TO_EXP2).astype(jnp.bfloat16) for part in s], axis=1)
            v = with_ones(listed(i, slice(INNER + at, INNER + at + HD)))
            both = jnp.dot(p, v, preferred_element_type=jnp.float32)
            keep = jnp.exp2((old_peak - peak) * TO_EXP2)
            total = total_ref[rows, here] * keep + both[:, HD:]
            acc = acc_ref[rows, here] * keep + both[:, :HD]
            attended[rows, here] = (acc / total).astype(jnp.bfloat16)
    for c in range(0, wo_ref.shape[1], 2 * PAIR):
        cols = slice(c, c + 2 * PAIR)
        out = jnp.dot(attended[...], wo_ref[:, cols], preferred_element_type=jnp.float32)
        y = (x_ref[:, cols].astype(jnp.float32) + mod_ref[2, :, cols] * out).astype(jnp.bfloat16)
        for n, y_ref in enumerate(ys):
            rows = tokens // pieces
            y_ref[:, cols] = y[n * rows : (n + 1) * rows]
    send_asked(count, asked, key_ref, ys, sends)


def last_part(count, late, asked, pieces, key_blocks, block_counts, early, blocks, q, state, x, mod, w, wo):
    part = jax.ShapeDtypeStruct((BLK, x.shape[1]), x.dtype)
    piece = jax.ShapeDtypeStruct((x.shape[0] // pieces, x.shape[1]), x.dtype)
    slots = len(early) + len(late)
    return pl.pallas_call(
        functools.partial(last_kernel, count, (EARLY,) * len(early), late, asked, pieces),
        out_shape=[piece] * pieces + [part] * len(asked),
        in_specs=[IN_SMEM] * 2 + [IN_VMEM] * (8 + slots),
        out_specs=[IN_VMEM] * (pieces + len(asked)),
        scratch_shapes=[
            pltpu.VMEM((slots * BLK, w.shape[0]), jnp.bfloat16),
            pltpu.VMEM((slots * BLK, 2 * INNER), jnp.bfloat16),
            pltpu.VMEM((x.shape[0], INNER), jnp.bfloat16),
        ],
        compiler_params=pltpu.CompilerParams(vmem_limit_bytes=LIMIT),
        name="last_part",
    )(key_blocks, block_counts, *early, *blocks, q, *state, x, mod, w, wo)


def on_device(activations, qkv_weight, out_weight, modulation, key_blocks, block_counts):
    count = lax.axis_size("seq")
    sections = lax.axis_size("section")
    x, w, wo = activations[0], qkv_weight[0], out_weight[0]
    mod = modulation.reshape(modulation.shape[1], 1, modulation.shape[2])
    key_blocks = key_blocks.T
    lists_of = (key_blocks, block_counts)
    here = [(s, s) for s in range(sections)]
    onward = [(s, (s + 1) % sections) for s in range(sections)]

    def exchange(send, i, hops):
        pairs = [(s * count + a, t * count + b) for s, t in hops for a, b in pairs_of(i, count)]
        return lax.ppermute(send, ("section", "seq"), pairs)

    order = (EARLY,) + LATE
    got = {i: exchange(send, i, here) for i, send in zip(order, pick_blocks([x], key_blocks, count, order))}
    q, *state, w = first_part(x, mod, w)
    early = [arrived_part(count, (EARLY,), x.shape[0] // BLK, *lists_of, [got[EARLY]], mod, w)]
    blocks = [got[i] for i in LATE]
    made = last_part(count, LATE, DIRECT, PIECES, *lists_of, early, blocks, q, state, x, mod, w, wo)
    pieces, sends = made[:PIECES], made[PIECES:]

    pieces = [lax.ppermute(piece, "section", onward) for piece in pieces]
    got = {i: exchange(send, i, onward) for i, send in zip(DIRECT, sends)}
    qkv = half_part(pieces[0], mod, w)
    pieces[1], qkv = lax.optimization_barrier((pieces[1], qkv))
    relayed = tuple(i for i in order if i not in DIRECT)
    params = pltpu.CompilerParams(vmem_limit_bytes=LIMIT)
    sends = pick_blocks(pieces, key_blocks, count, relayed, params)
    got.update({i: exchange(send, i, here) for i, send in zip(relayed, sends)})
    x, q, *state = second_part(*pieces, qkv, mod, w)
    early = [arrived_part(count, (EARLY,), x.shape[0] // BLK, *lists_of, [got[EARLY]], mod, w)]
    blocks = [got[i] for i in LATE]
    (out,) = last_part(count, LATE, (), 1, *lists_of, early, blocks, q, state, x, mod, w, wo)
    return out[None]


def solution(mesh):
    return jax.shard_map(
        on_device,
        mesh=mesh,
        in_specs=(
            P("section", "seq", None),
            P("section", None, None),
            P("section", None, None),
            P("section", None, None),
            P(),
            P(),
        ),
        out_specs=P("section", "seq", None),
        check_vma=False,
    )
```

```python
import functools

import jax
import jax.numpy as jnp
from jax import lax
from jax.experimental import pallas as pl
from jax.experimental.pallas import tpu as pltpu
from jax.sharding import PartitionSpec as P

HEADS = 12
HD = 128
BLK = 128
EPSILON = 1e-06
INNER = HEADS * HD
PAIR = 2 * HD
TO_EXP2 = HD ** (-0.5) * 1.4426950408889634
MASKED = -1e30
FIRST_EARLY, FIRST_LATE = (1,), (0, 2, 3)
SECOND_EARLY, SECOND_LATE = (1, 2, 3), (0,)
SWAPPED = (1,)
PIECES = 2
LIMIT = 16 * 2**20
FIRST_LIMIT = 30 * 2**20

IN_VMEM = pl.BlockSpec(memory_space=pltpu.VMEM)
IN_SMEM = pl.BlockSpec(memory_space=pltpu.SMEM)
IN_HBM = pl.BlockSpec(memory_space=pltpu.HBM)


def beyond(me, count):
    one = me + 1 - 2 * (me % 2)
    other_one = me - 1 + 2 * (me % 2)
    two = me + 2 - 4 * ((me // 2) % 2)
    other_two = me - 2 + 4 * ((me // 2) % 2)
    return [one, other_one, two, other_two]


def partner_table(count):
    table = []
    for me in range(count):
        table.append([p if 0 <= p < count else me for p in beyond(me, count)])
    return table


def pairs_of(exchange, count):
    table = partner_table(count)
    return [(me, table[me][exchange]) for me in range(count)]


def asked_block(key_ref, target, me, blocks_here):
    width = key_ref.shape[0]
    found = jnp.int32(0)
    for row in range(blocks_here):
        for entry in range(width):
            named = key_ref[entry, target * blocks_here + row]
            mine = (named >= me * blocks_here) & (named < (me + 1) * blocks_here)
            found = jnp.where(mine, named - me * blocks_here, found)
    return found


def partners_here(me, count):
    out = []
    for p in beyond(me, count):
        out.append(jnp.where((p >= 0) & (p < count), p, me))
    return out


def pick_kernel(count, exchanges, parts, key_ref, *refs):
    send_asked(count, exchanges, key_ref, refs[:parts], refs[parts:])


def pick_blocks(parts, key_blocks, count, exchanges, params=None):
    width = parts[0].shape[1]
    return pl.pallas_call(
        functools.partial(pick_kernel, count, exchanges, len(parts)),
        out_shape=[jax.ShapeDtypeStruct((BLK, width), parts[0].dtype)] * len(exchanges),
        in_specs=[IN_SMEM] + [IN_VMEM] * len(parts),
        out_specs=[IN_VMEM] * len(exchanges),
        compiler_params=params,
        name="pick_blocks",
    )(key_blocks, *parts)


def send_asked(count, exchanges, key_ref, parts, sends):
    me = lax.axis_index("seq")
    rows = parts[0].shape[0]
    blocks_here = len(parts) * rows // BLK
    for exchange, send in zip(exchanges, sends):
        block = asked_block(key_ref, partners_here(me, count)[exchange], me, blocks_here)
        if len(parts) == 1:
            send[...] = parts[0][pl.ds(pl.multiple_of(block * BLK, BLK), BLK), :]
        else:
            each = BLK // rows
            for n in range(blocks_here):

                @pl.when(block == n)
                def _():
                    for m in range(each):
                        send[m * rows : (m + 1) * rows, :] = parts[n * each + m][...]


def norm_rows(x_ref, mod_ref, out_ref, out_row):
    rows, width = x_ref.shape
    shift = mod_ref[0]
    scale = 1.0 + mod_ref[1]
    step = 16
    for r in range(0, rows, step):
        values = x_ref[r : r + step, :].astype(jnp.float32)
        center = jnp.sum(values, axis=-1, keepdims=True) * (1.0 / width)
        values = values - center
        spread = jnp.sum(values * values, axis=-1, keepdims=True) * (1.0 / width)
        normed = values * lax.rsqrt(spread + EPSILON)
        out_ref[out_row + r : out_row + r + step, :] = (normed * scale + shift).astype(jnp.bfloat16)


def project(source, weight_ref, column, width):
    return jnp.dot(
        source, weight_ref[:, column : column + width], preferred_element_type=jnp.float32
    ).astype(jnp.bfloat16)


def scores_of(q, k):
    return lax.dot_general(q, k, (((1,), (1,)), ((), ())), preferred_element_type=jnp.float32)


def with_ones(v):
    return jnp.concatenate([v, jnp.ones(v.shape, v.dtype)], axis=1)


def own_columns():
    wide = 4 * HD
    for at in range(0, INNER, wide):
        yield at, wide


def own_heads(normed, w_ref, q_ref, kv, peak_ref, total_ref, acc_ref, row, before):
    rows = slice(row, q_ref.shape[0])
    for n, (at, wide) in enumerate(own_columns()):
        cols = slice(at, at + wide)
        before(3 * n)
        q_ref[rows, cols] = project(normed[...], w_ref, at, wide)
        before(3 * n + 1)
        kv[rows, cols] = project(normed[...], w_ref, INNER + at, wide)
        before(3 * n + 2)
        kv[rows, INNER + at : INNER + at + wide] = project(normed[...], w_ref, 2 * INNER + at, wide)
        for h in range(at, at + wide, HD):
            here = slice(h, h + HD)
            s = scores_of(q_ref[:, here], kv[:, here])
            peak = jnp.max(s, axis=-1, keepdims=True)
            p = jnp.exp2((s - peak) * TO_EXP2).astype(jnp.bfloat16)
            both = jnp.dot(p, with_ones(kv[:, INNER + h : INNER + h + HD]), preferred_element_type=jnp.float32)
            peak_ref[:, here] = jnp.broadcast_to(peak, (s.shape[0], HD))
            total_ref[:, here] = both[:, HD:]
            acc_ref[:, here] = both[:, :HD]


def first_kernel(
    x_ref, mod_ref, w_hbm, q_ref, peak_ref, total_ref, acc_ref, w_ref, normed, kv, sems
):
    wide = 4 * HD
    copies = []
    for at in range(0, INNER, wide):
        for c in (at, INNER + at, 2 * INNER + at):
            n = len(copies)
            cols = slice(c, c + wide)
            copies.append(pltpu.make_async_copy(w_hbm.at[:, cols], w_ref.at[:, cols], sems.at[n]))
            copies[n].start()
    norm_rows(x_ref, mod_ref, normed, 0)
    own_heads(normed, w_ref, q_ref, kv, peak_ref, total_ref, acc_ref, 0, lambda n: copies[n].wait())


def own_scratch(tokens, width):
    return [pltpu.VMEM((tokens, width), jnp.bfloat16), pltpu.VMEM((tokens, 2 * INNER), jnp.bfloat16)]


def first_part(x, mod, w):
    tokens, width = x.shape
    state = jax.ShapeDtypeStruct((tokens, INNER), jnp.float32)
    held = [jax.ShapeDtypeStruct(shape, jnp.bfloat16) for shape in [(tokens, INNER), w.shape]]
    return pl.pallas_call(
        first_kernel,
        out_shape=held[:1] + [state] * 3 + held[1:],
        in_specs=[IN_VMEM, IN_VMEM, IN_HBM],
        out_specs=[IN_VMEM] * 5,
        scratch_shapes=own_scratch(tokens, width) + [pltpu.SemaphoreType.DMA((w.shape[1] // (2 * PAIR),))],
        compiler_params=pltpu.CompilerParams(vmem_limit_bytes=FIRST_LIMIT),
        name="first_part",
    )(x, mod, w)


def half_kernel(x_ref, mod_ref, w_ref, qkv_ref, normed):
    norm_rows(x_ref, mod_ref, normed, 0)
    for c in range(0, 3 * INNER, 4 * HD):
        qkv_ref[:, c : c + 4 * HD] = project(normed[...], w_ref, c, 4 * HD)


def half_part(x, mod, w):
    rows, width = x.shape
    return pl.pallas_call(
        half_kernel,
        out_shape=jax.ShapeDtypeStruct((rows, w.shape[1]), jnp.bfloat16),
        in_specs=[IN_VMEM] * 3,
        out_specs=IN_VMEM,
        scratch_shapes=[pltpu.VMEM((rows, width), jnp.bfloat16)],
        compiler_params=pltpu.CompilerParams(vmem_limit_bytes=LIMIT),
        name="half_part",
    )(x, mod, w)


def second_kernel(a_ref, b_ref, qkv_ref, mod_ref, w_ref, x_ref, q_ref, peak_ref, total_ref, acc_ref, normed, kv):
    rows = a_ref.shape[0]
    x_ref[:rows, :] = a_ref[...]
    x_ref[rows:, :] = b_ref[...]
    q_ref[:rows, :] = qkv_ref[:, :INNER]
    kv[:rows, :] = qkv_ref[:, INNER:]
    norm_rows(b_ref, mod_ref, normed, 0)
    own_heads(normed, w_ref, q_ref, kv, peak_ref, total_ref, acc_ref, rows, lambda n: None)


def second_part(a, b, qkv, mod, w):
    tokens, width = a.shape[0] + b.shape[0], a.shape[1]
    state = jax.ShapeDtypeStruct((tokens, INNER), jnp.float32)
    half = [jax.ShapeDtypeStruct(shape, jnp.bfloat16) for shape in ((tokens, width), (tokens, INNER))]
    return pl.pallas_call(
        second_kernel,
        out_shape=half + [state] * 3,
        in_specs=[IN_VMEM] * 5,
        out_specs=[IN_VMEM] * 5,
        scratch_shapes=[
            pltpu.VMEM(b.shape, jnp.bfloat16),
            pltpu.VMEM((tokens, 2 * INNER), jnp.bfloat16),
        ],
        compiler_params=pltpu.CompilerParams(vmem_limit_bytes=LIMIT),
        name="second_part",
    )(a, b, qkv, mod, w)


def uses(key_ref, count_ref, me, owner, blocks_here):
    used = jnp.bool_(False)
    for i in range(blocks_here):
        row = me * blocks_here + i
        for j in range(blocks_here, key_ref.shape[0]):
            used = used | ((key_ref[j, row] // blocks_here == owner) & (j < count_ref[row]))
    return used & (owner != me)


def project_block(block_ref, mod_ref, w_ref, normed, row, kv_ref):
    rows = slice(row, row + BLK)
    norm_rows(block_ref, mod_ref, normed, row)
    for c in range(0, 2 * INNER, 2 * PAIR):
        kv_ref[rows, c : c + 2 * PAIR] = project(normed[rows, :], w_ref, INNER + c, 2 * PAIR)


def arrived_kernel(count, exchanges, blocks_here, key_ref, count_ref, *rest):
    blocks, (mod_ref, w_ref, kv_ref, normed) = rest[: len(exchanges)], rest[len(exchanges) :]
    me = lax.axis_index("seq")
    partners = partners_here(me, count)
    for n, exchange in enumerate(exchanges):

        @pl.when(uses(key_ref, count_ref, me, partners[exchange], blocks_here))
        def _():
            project_block(blocks[n], mod_ref, w_ref, normed, n * BLK, kv_ref)


def arrived_part(count, exchanges, blocks_here, key_blocks, block_counts, blocks, mod, w):
    rows = len(exchanges) * BLK
    return pl.pallas_call(
        functools.partial(arrived_kernel, count, exchanges, blocks_here),
        out_shape=jax.ShapeDtypeStruct((rows, 2 * INNER), jnp.bfloat16),
        in_specs=[IN_SMEM] * 2 + [IN_VMEM] * (len(blocks) + 2),
        out_specs=IN_VMEM,
        scratch_shapes=[pltpu.VMEM((rows, w.shape[0]), jnp.bfloat16)],
        compiler_params=pltpu.CompilerParams(vmem_limit_bytes=LIMIT),
        name="arrived_part",
    )(key_blocks, block_counts, *blocks, mod, w)


def last_kernel(count, early, late, asked, pieces, key_ref, count_ref, *rest):
    early_ref, *rest = rest
    blocks, rest = rest[: len(late)], rest[len(late) :]
    q_ref, peak_ref, total_ref, acc_ref, x_ref, mod_ref, w_ref, wo_ref, *rest = rest
    if pieces == 1:
        y_out, normed, kv, attended, y_ref, sems = rest
        ys, sends, copies = [y_ref], [], []
    else:
        ys, sends, (normed, kv, attended) = rest[:pieces], rest[pieces:-3], rest[-3:]
    me = lax.axis_index("seq")
    tokens = x_ref.shape[0]
    blocks_here = tokens // BLK
    remote = key_ref.shape[0] - blocks_here
    partners = partners_here(me, count)
    slots = early + late
    for n, exchange in enumerate(slots):

        @pl.when(uses(key_ref, count_ref, me, partners[exchange], blocks_here))
        def _():
            if n < len(early):
                kv[n * BLK : (n + 1) * BLK, :] = early_ref[n * BLK : (n + 1) * BLK, :]
            else:
                project_block(blocks[n - len(early)], mod_ref, w_ref, normed, n * BLK, kv)

    starts, bias = [], []
    for i in range(blocks_here):
        row = me * blocks_here + i
        starts.append([])
        bias.append([])
        for j in range(remote):
            live = blocks_here + j < count_ref[row]
            bias[i].append(jnp.where(live, 0.0, MASKED))
            owner = key_ref[blocks_here + j, row] // blocks_here
            owner = jnp.where(live, owner, key_ref[blocks_here, row] // blocks_here)
            start = jnp.int32(0)
            for n, exchange in enumerate(slots):
                start = jnp.where(owner == partners[exchange], n * BLK, start)
            starts[i].append(pl.multiple_of(start, BLK))

    def listed(i, cols):
        return jnp.concatenate([kv[pl.ds(start, BLK), cols] for start in starts[i]], axis=0)

    for at in range(0, INNER, HD):
        here = slice(at, at + HD)
        for i in range(blocks_here):
            rows = slice(i * BLK, (i + 1) * BLK)
            s = scores_of(q_ref[rows, here], listed(i, here))
            s = [s[:, j * BLK : (j + 1) * BLK] + bias[i][j] for j in range(remote)]
            old_peak = peak_ref[rows, here]
            peak = old_peak
            for part in s:
                peak = jnp.maximum(peak, jnp.max(part, axis=-1, keepdims=True))
            p = jnp.concatenate([jnp.exp2((part - peak) * TO_EXP2).astype(jnp.bfloat16) for part in s], axis=1)
            v = with_ones(listed(i, slice(INNER + at, INNER + at + HD)))
            both = jnp.dot(p, v, preferred_element_type=jnp.float32)
            keep = jnp.exp2((old_peak - peak) * TO_EXP2)
            total = total_ref[rows, here] * keep + both[:, HD:]
            acc = acc_ref[rows, here] * keep + both[:, :HD]
            attended[rows, here] = (acc / total).astype(jnp.bfloat16)
    for c in range(0, wo_ref.shape[1], 2 * PAIR):
        cols = slice(c, c + 2 * PAIR)
        out = jnp.dot(attended[...], wo_ref[:, cols], preferred_element_type=jnp.float32)
        y = (x_ref[:, cols].astype(jnp.float32) + mod_ref[2, :, cols] * out).astype(jnp.bfloat16)
        for n, y_ref in enumerate(ys):
            rows = tokens // pieces
            y_ref[:, cols] = y[n * rows : (n + 1) * rows]
        if pieces == 1:
            copies.append(pltpu.make_async_copy(ys[0].at[:, cols], y_out.at[:, cols], sems.at[len(copies)]))
            copies[-1].start()
    send_asked(count, asked, key_ref, ys, sends)
    if pieces == 1:
        for copy in copies:
            copy.wait()


def last_part(count, early, late, asked, pieces, key_blocks, block_counts, early_kv, blocks, q, state, x, mod, w, wo):
    part = jax.ShapeDtypeStruct((BLK, x.shape[1]), x.dtype)
    piece = jax.ShapeDtypeStruct((x.shape[0] // pieces, x.shape[1]), x.dtype)
    slots = len(early) + len(late)
    written = []
    if pieces == 1:
        written = [pltpu.VMEM(x.shape, x.dtype), pltpu.SemaphoreType.DMA((wo.shape[1] // (2 * PAIR),))]
    return pl.pallas_call(
        functools.partial(last_kernel, count, early, late, asked, pieces),
        out_shape=[piece] * pieces + [part] * len(asked),
        in_specs=[IN_SMEM] * 2 + [IN_VMEM] * (9 + len(late)),
        out_specs=[IN_HBM] if pieces == 1 else [IN_VMEM] * (pieces + len(asked)),
        scratch_shapes=[
            pltpu.VMEM((slots * BLK, w.shape[0]), jnp.bfloat16),
            pltpu.VMEM((slots * BLK, 2 * INNER), jnp.bfloat16),
            pltpu.VMEM((x.shape[0], INNER), jnp.bfloat16),
        ]
        + written,
        compiler_params=pltpu.CompilerParams(vmem_limit_bytes=LIMIT),
        name="last_part",
    )(key_blocks, block_counts, early_kv, *blocks, q, *state, x, mod, w, wo)


def on_device(activations, qkv_weight, out_weight, modulation, key_blocks, block_counts):
    count = lax.axis_size("seq")
    sections = lax.axis_size("section")
    x, w, wo = activations[0], qkv_weight[0], out_weight[0]
    mod = modulation.reshape(modulation.shape[1], 1, modulation.shape[2])
    key_blocks = key_blocks.T
    lists_of = (key_blocks, block_counts)
    here = [(s, s) for s in range(sections)]
    onward = [(s, (s + 1) % sections) for s in range(sections)]

    def exchange(send, i, hops):
        pairs = [(s * count + a, t * count + b) for s, t in hops for a, b in pairs_of(i, count)]
        return lax.ppermute(send, ("section", "seq"), pairs)

    order = FIRST_EARLY + FIRST_LATE
    blocks_here = x.shape[0] // BLK
    got = {i: exchange(send, i, here) for i, send in zip(order, pick_blocks([x], key_blocks, count, order))}
    q, *state, w = first_part(x, mod, w)
    early = arrived_part(count, FIRST_EARLY, blocks_here, *lists_of, [got[i] for i in FIRST_EARLY], mod, w)
    blocks = [got[i] for i in FIRST_LATE]
    made = last_part(
        count, FIRST_EARLY, FIRST_LATE, SWAPPED, PIECES, *lists_of, early, blocks, q, state, x, mod, w, wo
    )
    pieces, sends = made[:PIECES], made[PIECES:]

    pieces = [lax.ppermute(piece, "section", onward) for piece in pieces]
    swapped = [exchange(send, i, here) for i, send in zip(SWAPPED, sends)]
    got = {i: lax.ppermute(block, "section", onward) for i, block in zip(SWAPPED, swapped)}
    qkv = half_part(pieces[0], mod, w)
    pieces[1], qkv = lax.optimization_barrier((pieces[1], qkv))
    relayed = tuple(i for i in order if i not in SWAPPED)
    params = pltpu.CompilerParams(vmem_limit_bytes=LIMIT)
    sends = pick_blocks(pieces, key_blocks, count, relayed, params)
    got.update({i: exchange(send, i, here) for i, send in zip(relayed, sends)})
    x, q, *state = second_part(*pieces, qkv, mod, w)
    early = arrived_part(count, SECOND_EARLY, blocks_here, *lists_of, [got[i] for i in SECOND_EARLY], mod, w)
    blocks = [got[i] for i in SECOND_LATE]
    (out,) = last_part(
        count, SECOND_EARLY, SECOND_LATE, (), 1, *lists_of, early, blocks, q, state, x, mod, w, wo
    )
    return out[None]


def solution(mesh):
    return jax.shard_map(
        on_device,
        mesh=mesh,
        in_specs=(
            P("section", "seq", None),
            P("section", None, None),
            P("section", None, None),
            P("section", None, None),
            P(),
            P(),
        ),
        out_specs=P("section", "seq", None),
        check_vma=False,
    )
```

```python
import functools

import jax
import jax.numpy as jnp
from jax import lax
from jax.experimental import pallas as pl
from jax.experimental.pallas import tpu as pltpu
from jax.sharding import PartitionSpec as P

HEADS = 12
HD = 128
BLK = 128
EPSILON = 1e-06
INNER = HEADS * HD
PAIR = 2 * HD
TO_EXP2 = HD ** (-0.5) * 1.4426950408889634
MASKED = -1e30
FIRST_EARLY, FIRST_LATE = (1,), (0, 2, 3)
SECOND_EARLY, SECOND_LATE = (0, 2, 1), (3,)
SWAPPED = (1,)
PIECES = 2
LIMIT = 16 * 2**20
FIRST_LIMIT = 30 * 2**20

IN_VMEM = pl.BlockSpec(memory_space=pltpu.VMEM)
IN_SMEM = pl.BlockSpec(memory_space=pltpu.SMEM)
IN_HBM = pl.BlockSpec(memory_space=pltpu.HBM)


def beyond(me, count):
    one = me + 1 - 2 * (me % 2)
    other_one = me - 1 + 2 * (me % 2)
    two = me + 2 - 4 * ((me // 2) % 2)
    other_two = me - 2 + 4 * ((me // 2) % 2)
    return [one, other_one, two, other_two]


def partner_table(count):
    table = []
    for me in range(count):
        table.append([p if 0 <= p < count else me for p in beyond(me, count)])
    return table


def pairs_of(exchange, count):
    table = partner_table(count)
    return [(me, table[me][exchange]) for me in range(count)]


def asked_block(key_ref, target, me, blocks_here):
    width = key_ref.shape[0]
    found = jnp.int32(0)
    for row in range(blocks_here):
        for entry in range(width):
            named = key_ref[entry, target * blocks_here + row]
            mine = (named >= me * blocks_here) & (named < (me + 1) * blocks_here)
            found = jnp.where(mine, named - me * blocks_here, found)
    return found


def partners_here(me, count):
    out = []
    for p in beyond(me, count):
        out.append(jnp.where((p >= 0) & (p < count), p, me))
    return out


def pick_kernel(count, exchanges, parts, key_ref, *refs):
    send_asked(count, exchanges, key_ref, refs[:parts], refs[parts:])


def pick_blocks(parts, key_blocks, count, exchanges, params=None):
    width = parts[0].shape[1]
    return pl.pallas_call(
        functools.partial(pick_kernel, count, exchanges, len(parts)),
        out_shape=[jax.ShapeDtypeStruct((BLK, width), parts[0].dtype)] * len(exchanges),
        in_specs=[IN_SMEM] + [IN_VMEM] * len(parts),
        out_specs=[IN_VMEM] * len(exchanges),
        compiler_params=params,
        name="pick_blocks",
    )(key_blocks, *parts)


def send_asked(count, exchanges, key_ref, parts, sends):
    me = lax.axis_index("seq")
    rows = parts[0].shape[0]
    blocks_here = len(parts) * rows // BLK
    for exchange, send in zip(exchanges, sends):
        block = asked_block(key_ref, partners_here(me, count)[exchange], me, blocks_here)
        if len(parts) == 1:
            send[...] = parts[0][pl.ds(pl.multiple_of(block * BLK, BLK), BLK), :]
        else:
            each = BLK // rows
            for n in range(blocks_here):

                @pl.when(block == n)
                def _():
                    for m in range(each):
                        send[m * rows : (m + 1) * rows, :] = parts[n * each + m][...]


def norm_rows(x_ref, mod_ref, out_ref, out_row):
    rows, width = x_ref.shape
    shift = mod_ref[0]
    scale = 1.0 + mod_ref[1]
    step = 16
    for r in range(0, rows, step):
        values = x_ref[r : r + step, :].astype(jnp.float32)
        center = jnp.sum(values, axis=-1, keepdims=True) * (1.0 / width)
        values = values - center
        spread = jnp.sum(values * values, axis=-1, keepdims=True) * (1.0 / width)
        normed = values * lax.rsqrt(spread + EPSILON)
        out_ref[out_row + r : out_row + r + step, :] = (normed * scale + shift).astype(jnp.bfloat16)


def project(source, weight_ref, column, width):
    return jnp.dot(
        source, weight_ref[:, column : column + width], preferred_element_type=jnp.float32
    ).astype(jnp.bfloat16)


def scores_of(q, k):
    return lax.dot_general(q, k, (((1,), (1,)), ((), ())), preferred_element_type=jnp.float32)


def with_ones(v):
    return jnp.concatenate([v, jnp.ones(v.shape, v.dtype)], axis=1)


def own_columns():
    wide = 4 * HD
    for at in range(0, INNER, wide):
        yield at, wide


def own_heads(normed, w_ref, q_ref, kv, peak_ref, total_ref, acc_ref, row, before):
    rows = slice(row, q_ref.shape[0])
    for n, (at, wide) in enumerate(own_columns()):
        cols = slice(at, at + wide)
        before(3 * n)
        q_ref[rows, cols] = project(normed[...], w_ref, at, wide)
        before(3 * n + 1)
        kv[rows, cols] = project(normed[...], w_ref, INNER + at, wide)
        before(3 * n + 2)
        kv[rows, INNER + at : INNER + at + wide] = project(normed[...], w_ref, 2 * INNER + at, wide)
        for h in range(at, at + wide, HD):
            here = slice(h, h + HD)
            s = scores_of(q_ref[:, here], kv[:, here])
            peak = jnp.max(s, axis=-1, keepdims=True)
            p = jnp.exp2((s - peak) * TO_EXP2).astype(jnp.bfloat16)
            both = jnp.dot(p, with_ones(kv[:, INNER + h : INNER + h + HD]), preferred_element_type=jnp.float32)
            peak_ref[:, here] = jnp.broadcast_to(peak, (s.shape[0], HD))
            total_ref[:, here] = both[:, HD:]
            acc_ref[:, here] = both[:, :HD]


def first_kernel(
    x_ref, mod_ref, w_hbm, q_ref, peak_ref, total_ref, acc_ref, w_ref, normed, kv, sems
):
    wide = 4 * HD
    copies = []
    for at in range(0, INNER, wide):
        for c in (at, INNER + at, 2 * INNER + at):
            n = len(copies)
            cols = slice(c, c + wide)
            copies.append(pltpu.make_async_copy(w_hbm.at[:, cols], w_ref.at[:, cols], sems.at[n]))
            copies[n].start()
    norm_rows(x_ref, mod_ref, normed, 0)
    own_heads(normed, w_ref, q_ref, kv, peak_ref, total_ref, acc_ref, 0, lambda n: copies[n].wait())


def own_scratch(tokens, width):
    return [pltpu.VMEM((tokens, width), jnp.bfloat16), pltpu.VMEM((tokens, 2 * INNER), jnp.bfloat16)]


def first_part(x, mod, w):
    tokens, width = x.shape
    state = jax.ShapeDtypeStruct((tokens, INNER), jnp.float32)
    held = [jax.ShapeDtypeStruct(shape, jnp.bfloat16) for shape in [(tokens, INNER), w.shape]]
    return pl.pallas_call(
        first_kernel,
        out_shape=held[:1] + [state] * 3 + held[1:],
        in_specs=[IN_VMEM, IN_VMEM, IN_HBM],
        out_specs=[IN_VMEM] * 5,
        scratch_shapes=own_scratch(tokens, width) + [pltpu.SemaphoreType.DMA((w.shape[1] // (2 * PAIR),))],
        compiler_params=pltpu.CompilerParams(vmem_limit_bytes=FIRST_LIMIT),
        name="first_part",
    )(x, mod, w)


def half_kernel(x_ref, mod_ref, w_ref, qkv_ref, normed):
    norm_rows(x_ref, mod_ref, normed, 0)
    for c in range(0, 3 * INNER, 4 * HD):
        qkv_ref[:, c : c + 4 * HD] = project(normed[...], w_ref, c, 4 * HD)


def half_part(x, mod, w):
    rows, width = x.shape
    return pl.pallas_call(
        half_kernel,
        out_shape=jax.ShapeDtypeStruct((rows, w.shape[1]), jnp.bfloat16),
        in_specs=[IN_VMEM] * 3,
        out_specs=IN_VMEM,
        scratch_shapes=[pltpu.VMEM((rows, width), jnp.bfloat16)],
        compiler_params=pltpu.CompilerParams(vmem_limit_bytes=LIMIT),
        name="half_part",
    )(x, mod, w)


def second_kernel(a_ref, b_ref, qkv_ref, mod_ref, w_ref, x_ref, q_ref, peak_ref, total_ref, acc_ref, normed, kv):
    rows = a_ref.shape[0]
    x_ref[:rows, :] = a_ref[...]
    x_ref[rows:, :] = b_ref[...]
    q_ref[:rows, :] = qkv_ref[:, :INNER]
    kv[:rows, :] = qkv_ref[:, INNER:]
    norm_rows(b_ref, mod_ref, normed, 0)
    own_heads(normed, w_ref, q_ref, kv, peak_ref, total_ref, acc_ref, rows, lambda n: None)


def second_part(a, b, qkv, mod, w):
    tokens, width = a.shape[0] + b.shape[0], a.shape[1]
    state = jax.ShapeDtypeStruct((tokens, INNER), jnp.float32)
    half = [jax.ShapeDtypeStruct(shape, jnp.bfloat16) for shape in ((tokens, width), (tokens, INNER))]
    return pl.pallas_call(
        second_kernel,
        out_shape=half + [state] * 3,
        in_specs=[IN_VMEM] * 5,
        out_specs=[IN_VMEM] * 5,
        scratch_shapes=[
            pltpu.VMEM(b.shape, jnp.bfloat16),
            pltpu.VMEM((tokens, 2 * INNER), jnp.bfloat16),
        ],
        compiler_params=pltpu.CompilerParams(vmem_limit_bytes=LIMIT),
        name="second_part",
    )(a, b, qkv, mod, w)


def uses(key_ref, count_ref, me, owner, blocks_here):
    used = jnp.bool_(False)
    for i in range(blocks_here):
        row = me * blocks_here + i
        for j in range(blocks_here, key_ref.shape[0]):
            used = used | ((key_ref[j, row] // blocks_here == owner) & (j < count_ref[row]))
    return used & (owner != me)


def project_block(block_ref, mod_ref, w_ref, normed, row, kv_ref):
    rows = slice(row, row + BLK)
    norm_rows(block_ref, mod_ref, normed, row)
    for c in range(0, 2 * INNER, 2 * PAIR):
        kv_ref[rows, c : c + 2 * PAIR] = project(normed[rows, :], w_ref, INNER + c, 2 * PAIR)


def arrived_kernel(count, exchanges, blocks_here, key_ref, count_ref, *rest):
    blocks, (mod_ref, w_ref, kv_ref, normed) = rest[: len(exchanges)], rest[len(exchanges) :]
    me = lax.axis_index("seq")
    partners = partners_here(me, count)
    for n, exchange in enumerate(exchanges):

        @pl.when(uses(key_ref, count_ref, me, partners[exchange], blocks_here))
        def _():
            project_block(blocks[n], mod_ref, w_ref, normed, n * BLK, kv_ref)


def arrived_part(count, exchanges, blocks_here, key_blocks, block_counts, blocks, mod, w):
    rows = len(exchanges) * BLK
    return pl.pallas_call(
        functools.partial(arrived_kernel, count, exchanges, blocks_here),
        out_shape=jax.ShapeDtypeStruct((rows, 2 * INNER), jnp.bfloat16),
        in_specs=[IN_SMEM] * 2 + [IN_VMEM] * (len(blocks) + 2),
        out_specs=IN_VMEM,
        scratch_shapes=[pltpu.VMEM((rows, w.shape[0]), jnp.bfloat16)],
        compiler_params=pltpu.CompilerParams(vmem_limit_bytes=LIMIT),
        name="arrived_part",
    )(key_blocks, block_counts, *blocks, mod, w)


def last_kernel(count, early, late, asked, pieces, key_ref, count_ref, *rest):
    early_ref, *rest = rest
    blocks, rest = rest[: len(late)], rest[len(late) :]
    q_ref, peak_ref, total_ref, acc_ref, x_ref, mod_ref, w_ref, wo_ref, *rest = rest
    if pieces == 1:
        y_out, normed, kv, attended, y_ref, sems = rest
        ys, sends, copies = [y_ref], [], []
    else:
        ys, sends, (normed, kv, attended) = rest[:pieces], rest[pieces:-3], rest[-3:]
    me = lax.axis_index("seq")
    tokens = x_ref.shape[0]
    blocks_here = tokens // BLK
    remote = key_ref.shape[0] - blocks_here
    partners = partners_here(me, count)
    slots = early + late
    for n, exchange in enumerate(slots):

        @pl.when(uses(key_ref, count_ref, me, partners[exchange], blocks_here))
        def _():
            if n < len(early):
                kv[n * BLK : (n + 1) * BLK, :] = early_ref[n * BLK : (n + 1) * BLK, :]
            else:
                project_block(blocks[n - len(early)], mod_ref, w_ref, normed, n * BLK, kv)

    starts, bias = [], []
    for i in range(blocks_here):
        row = me * blocks_here + i
        starts.append([])
        bias.append([])
        for j in range(remote):
            live = blocks_here + j < count_ref[row]
            bias[i].append(jnp.where(live, 0.0, MASKED))
            owner = key_ref[blocks_here + j, row] // blocks_here
            owner = jnp.where(live, owner, key_ref[blocks_here, row] // blocks_here)
            start = jnp.int32(0)
            for n, exchange in enumerate(slots):
                start = jnp.where(owner == partners[exchange], n * BLK, start)
            starts[i].append(pl.multiple_of(start, BLK))

    def listed(i, cols):
        return jnp.concatenate([kv[pl.ds(start, BLK), cols] for start in starts[i]], axis=0)

    for at in range(0, INNER, HD):
        here = slice(at, at + HD)
        for i in range(blocks_here):
            rows = slice(i * BLK, (i + 1) * BLK)
            s = scores_of(q_ref[rows, here], listed(i, here))
            s = [s[:, j * BLK : (j + 1) * BLK] + bias[i][j] for j in range(remote)]
            old_peak = peak_ref[rows, here]
            peak = old_peak
            for part in s:
                peak = jnp.maximum(peak, jnp.max(part, axis=-1, keepdims=True))
            p = jnp.concatenate([jnp.exp2((part - peak) * TO_EXP2).astype(jnp.bfloat16) for part in s], axis=1)
            v = with_ones(listed(i, slice(INNER + at, INNER + at + HD)))
            both = jnp.dot(p, v, preferred_element_type=jnp.float32)
            keep = jnp.exp2((old_peak - peak) * TO_EXP2)
            total = total_ref[rows, here] * keep + both[:, HD:]
            acc = acc_ref[rows, here] * keep + both[:, :HD]
            attended[rows, here] = (acc / total).astype(jnp.bfloat16)
    for c in range(0, wo_ref.shape[1], 2 * PAIR):
        cols = slice(c, c + 2 * PAIR)
        out = jnp.dot(attended[...], wo_ref[:, cols], preferred_element_type=jnp.float32)
        y = (x_ref[:, cols].astype(jnp.float32) + mod_ref[2, :, cols] * out).astype(jnp.bfloat16)
        for n, y_ref in enumerate(ys):
            rows = tokens // pieces
            y_ref[:, cols] = y[n * rows : (n + 1) * rows]
        if pieces == 1:
            copies.append(pltpu.make_async_copy(ys[0].at[:, cols], y_out.at[:, cols], sems.at[len(copies)]))
            copies[-1].start()
    send_asked(count, asked, key_ref, ys, sends)
    if pieces == 1:
        for copy in copies:
            copy.wait()


def last_part(count, early, late, asked, pieces, key_blocks, block_counts, early_kv, blocks, q, state, x, mod, w, wo):
    part = jax.ShapeDtypeStruct((BLK, x.shape[1]), x.dtype)
    piece = jax.ShapeDtypeStruct((x.shape[0] // pieces, x.shape[1]), x.dtype)
    slots = len(early) + len(late)
    written = []
    if pieces == 1:
        written = [pltpu.VMEM(x.shape, x.dtype), pltpu.SemaphoreType.DMA((wo.shape[1] // (2 * PAIR),))]
    return pl.pallas_call(
        functools.partial(last_kernel, count, early, late, asked, pieces),
        out_shape=[piece] * pieces + [part] * len(asked),
        in_specs=[IN_SMEM] * 2 + [IN_VMEM] * (9 + len(late)),
        out_specs=[IN_HBM] if pieces == 1 else [IN_VMEM] * (pieces + len(asked)),
        scratch_shapes=[
            pltpu.VMEM((slots * BLK, w.shape[0]), jnp.bfloat16),
            pltpu.VMEM((slots * BLK, 2 * INNER), jnp.bfloat16),
            pltpu.VMEM((x.shape[0], INNER), jnp.bfloat16),
        ]
        + written,
        compiler_params=pltpu.CompilerParams(vmem_limit_bytes=LIMIT),
        name="last_part",
    )(key_blocks, block_counts, early_kv, *blocks, q, *state, x, mod, w, wo)


def on_device(activations, qkv_weight, out_weight, modulation, key_blocks, block_counts):
    count = lax.axis_size("seq")
    sections = lax.axis_size("section")
    x, w, wo = activations[0], qkv_weight[0], out_weight[0]
    mod = modulation.reshape(modulation.shape[1], 1, modulation.shape[2])
    key_blocks = key_blocks.T
    lists_of = (key_blocks, block_counts)
    here = [(s, s) for s in range(sections)]
    onward = [(s, (s + 1) % sections) for s in range(sections)]

    def exchange(send, i, hops):
        pairs = [(s * count + a, t * count + b) for s, t in hops for a, b in pairs_of(i, count)]
        return lax.ppermute(send, ("section", "seq"), pairs)

    order = FIRST_EARLY + FIRST_LATE
    blocks_here = x.shape[0] // BLK
    got = {i: exchange(send, i, here) for i, send in zip(order, pick_blocks([x], key_blocks, count, order))}
    q, *state, w = first_part(x, mod, w)
    early = arrived_part(count, FIRST_EARLY, blocks_here, *lists_of, [got[i] for i in FIRST_EARLY], mod, w)
    blocks = [got[i] for i in FIRST_LATE]
    made = last_part(
        count, FIRST_EARLY, FIRST_LATE, SWAPPED, PIECES, *lists_of, early, blocks, q, state, x, mod, w, wo
    )
    pieces, sends = made[:PIECES], made[PIECES:]

    pieces = [lax.ppermute(piece, "section", onward) for piece in pieces]
    swapped = [exchange(send, i, here) for i, send in zip(SWAPPED, sends)]
    got = {i: lax.ppermute(block, "section", onward) for i, block in zip(SWAPPED, swapped)}
    qkv = half_part(pieces[0], mod, w)
    pieces[1], qkv = lax.optimization_barrier((pieces[1], qkv))
    relayed = tuple(i for i in order if i not in SWAPPED)
    params = pltpu.CompilerParams(vmem_limit_bytes=LIMIT)
    sends = pick_blocks(pieces, key_blocks, count, relayed, params)
    got.update({i: exchange(send, i, here) for i, send in zip(relayed, sends)})
    x, q, *state = second_part(*pieces, qkv, mod, w)
    early = arrived_part(count, SECOND_EARLY, blocks_here, *lists_of, [got[i] for i in SECOND_EARLY], mod, w)
    blocks = [got[i] for i in SECOND_LATE]
    (out,) = last_part(
        count, SECOND_EARLY, SECOND_LATE, (), 1, *lists_of, early, blocks, q, state, x, mod, w, wo
    )
    return out[None]


def solution(mesh):
    return jax.shard_map(
        on_device,
        mesh=mesh,
        in_specs=(
            P("section", "seq", None),
            P("section", None, None),
            P("section", None, None),
            P("section", None, None),
            P(),
            P(),
        ),
        out_specs=P("section", "seq", None),
        check_vma=False,
    )
```

```python
import functools

import jax
import jax.numpy as jnp
from jax import lax
from jax.experimental import pallas as pl
from jax.experimental.pallas import tpu as pltpu
from jax.sharding import PartitionSpec as P

HEADS = 12
HD = 128
BLK = 128
EPSILON = 1e-06
INNER = HEADS * HD
PAIR = 2 * HD
TO_EXP2 = HD ** (-0.5) * 1.4426950408889634
MASKED = -1e30
FIRST_EARLY, FIRST_LATE = (1,), (0, 2, 3)
SECOND_EARLY, SECOND_LATE = (0, 2, 1), (3,)
SWAPPED = (1,)
PIECES = 2
LIMIT = 16 * 2**20
FIRST_LIMIT = 30 * 2**20

IN_VMEM = pl.BlockSpec(memory_space=pltpu.VMEM)
IN_SMEM = pl.BlockSpec(memory_space=pltpu.SMEM)
IN_HBM = pl.BlockSpec(memory_space=pltpu.HBM)


def beyond(me, count):
    one = me + 1 - 2 * (me % 2)
    other_one = me - 1 + 2 * (me % 2)
    two = me + 2 - 4 * ((me // 2) % 2)
    other_two = me - 2 + 4 * ((me // 2) % 2)
    return [one, other_one, two, other_two]


def partner_table(count):
    table = []
    for me in range(count):
        table.append([p if 0 <= p < count else me for p in beyond(me, count)])
    return table


def pairs_of(exchange, count):
    table = partner_table(count)
    return [(me, table[me][exchange]) for me in range(count)]


def asked_block(key_ref, target, me, blocks_here):
    width = key_ref.shape[0]
    found = jnp.int32(0)
    for row in range(blocks_here):
        for entry in range(width):
            named = key_ref[entry, target * blocks_here + row]
            mine = (named >= me * blocks_here) & (named < (me + 1) * blocks_here)
            found = jnp.where(mine, named - me * blocks_here, found)
    return found


def partners_here(me, count):
    out = []
    for p in beyond(me, count):
        out.append(jnp.where((p >= 0) & (p < count), p, me))
    return out


def pick_kernel(count, exchanges, parts, key_ref, *refs):
    send_asked(count, exchanges, key_ref, refs[:parts], refs[parts:])


def pick_blocks(parts, key_blocks, count, exchanges, params=None):
    width = parts[0].shape[1]
    return pl.pallas_call(
        functools.partial(pick_kernel, count, exchanges, len(parts)),
        out_shape=[jax.ShapeDtypeStruct((BLK, width), parts[0].dtype)] * len(exchanges),
        in_specs=[IN_SMEM] + [IN_VMEM] * len(parts),
        out_specs=[IN_VMEM] * len(exchanges),
        compiler_params=params,
        name="pick_blocks",
    )(key_blocks, *parts)


def send_asked(count, exchanges, key_ref, parts, sends):
    me = lax.axis_index("seq")
    rows = parts[0].shape[0]
    blocks_here = len(parts) * rows // BLK
    for exchange, send in zip(exchanges, sends):
        block = asked_block(key_ref, partners_here(me, count)[exchange], me, blocks_here)
        if len(parts) == 1:
            send[...] = parts[0][pl.ds(pl.multiple_of(block * BLK, BLK), BLK), :]
        else:
            each = BLK // rows
            for n in range(blocks_here):

                @pl.when(block == n)
                def _():
                    for m in range(each):
                        send[m * rows : (m + 1) * rows, :] = parts[n * each + m][...]


def norm_rows(x_ref, mod_ref, out_ref, out_row):
    rows, width = x_ref.shape
    shift = mod_ref[0]
    scale = 1.0 + mod_ref[1]
    step = 16
    for r in range(0, rows, step):
        values = x_ref[r : r + step, :].astype(jnp.float32)
        center = jnp.sum(values, axis=-1, keepdims=True) * (1.0 / width)
        values = values - center
        spread = jnp.sum(values * values, axis=-1, keepdims=True) * (1.0 / width)
        normed = values * lax.rsqrt(spread + EPSILON)
        out_ref[out_row + r : out_row + r + step, :] = (normed * scale + shift).astype(jnp.bfloat16)


def project(source, weight_ref, column, width):
    return jnp.dot(
        source, weight_ref[:, column : column + width], preferred_element_type=jnp.float32
    ).astype(jnp.bfloat16)


def scores_of(q, k):
    return lax.dot_general(q, k, (((1,), (1,)), ((), ())), preferred_element_type=jnp.float32)


def with_ones(v):
    return jnp.concatenate([v, jnp.ones(v.shape, v.dtype)], axis=1)


def own_columns():
    wide = 4 * HD
    for at in range(0, INNER, wide):
        yield at, wide


def own_heads(normed, w_ref, q_ref, kv, peak_ref, total_ref, acc_ref, row, before):
    rows = slice(row, q_ref.shape[0])
    for n, (at, wide) in enumerate(own_columns()):
        cols = slice(at, at + wide)
        before(3 * n)
        q_ref[rows, cols] = project(normed[...], w_ref, at, wide)
        before(3 * n + 1)
        kv[rows, cols] = project(normed[...], w_ref, INNER + at, wide)
        before(3 * n + 2)
        kv[rows, INNER + at : INNER + at + wide] = project(normed[...], w_ref, 2 * INNER + at, wide)
        for h in range(at, at + wide, HD):
            here = slice(h, h + HD)
            s = scores_of(q_ref[:, here], kv[:, here])
            peak = jnp.max(s, axis=-1, keepdims=True)
            p = jnp.exp2((s - peak) * TO_EXP2).astype(jnp.bfloat16)
            both = jnp.dot(p, with_ones(kv[:, INNER + h : INNER + h + HD]), preferred_element_type=jnp.float32)
            peak_ref[:, here] = jnp.broadcast_to(peak, (s.shape[0], HD))
            total_ref[:, here] = both[:, HD:]
            acc_ref[:, here] = both[:, :HD]


def first_kernel(
    x_ref, mod_ref, w_hbm, q_ref, peak_ref, total_ref, acc_ref, w_ref, normed, kv, sems
):
    wide = 4 * HD
    copies = []
    for at in range(0, INNER, wide):
        for c in (at, INNER + at, 2 * INNER + at):
            n = len(copies)
            cols = slice(c, c + wide)
            copies.append(pltpu.make_async_copy(w_hbm.at[:, cols], w_ref.at[:, cols], sems.at[n]))
            copies[n].start()
    norm_rows(x_ref, mod_ref, normed, 0)
    own_heads(normed, w_ref, q_ref, kv, peak_ref, total_ref, acc_ref, 0, lambda n: copies[n].wait())


def own_scratch(tokens, width):
    return [pltpu.VMEM((tokens, width), jnp.bfloat16), pltpu.VMEM((tokens, 2 * INNER), jnp.bfloat16)]


def first_part(x, mod, w):
    tokens, width = x.shape
    state = jax.ShapeDtypeStruct((tokens, INNER), jnp.float32)
    held = [jax.ShapeDtypeStruct(shape, jnp.bfloat16) for shape in [(tokens, INNER), w.shape]]
    return pl.pallas_call(
        first_kernel,
        out_shape=held[:1] + [state] * 3 + held[1:],
        in_specs=[IN_VMEM, IN_VMEM, IN_HBM],
        out_specs=[IN_VMEM] * 5,
        scratch_shapes=own_scratch(tokens, width) + [pltpu.SemaphoreType.DMA((w.shape[1] // (2 * PAIR),))],
        compiler_params=pltpu.CompilerParams(vmem_limit_bytes=FIRST_LIMIT),
        name="first_part",
    )(x, mod, w)


def half_kernel(x_ref, mod_ref, w_ref, qkv_ref, normed):
    norm_rows(x_ref, mod_ref, normed, 0)
    for c in range(0, 3 * INNER, 4 * HD):
        qkv_ref[:, c : c + 4 * HD] = project(normed[...], w_ref, c, 4 * HD)


def half_part(x, mod, w):
    rows, width = x.shape
    return pl.pallas_call(
        half_kernel,
        out_shape=jax.ShapeDtypeStruct((rows, w.shape[1]), jnp.bfloat16),
        in_specs=[IN_VMEM] * 3,
        out_specs=IN_VMEM,
        scratch_shapes=[pltpu.VMEM((rows, width), jnp.bfloat16)],
        compiler_params=pltpu.CompilerParams(vmem_limit_bytes=LIMIT),
        name="half_part",
    )(x, mod, w)


def second_kernel(a_ref, b_ref, qkv_ref, mod_ref, w_ref, x_ref, q_ref, peak_ref, total_ref, acc_ref, normed, kv):
    rows = a_ref.shape[0]
    x_ref[:rows, :] = a_ref[...]
    x_ref[rows:, :] = b_ref[...]
    q_ref[:rows, :] = qkv_ref[:, :INNER]
    kv[:rows, :] = qkv_ref[:, INNER:]
    norm_rows(b_ref, mod_ref, normed, 0)
    own_heads(normed, w_ref, q_ref, kv, peak_ref, total_ref, acc_ref, rows, lambda n: None)


def second_part(a, b, qkv, mod, w):
    tokens, width = a.shape[0] + b.shape[0], a.shape[1]
    state = jax.ShapeDtypeStruct((tokens, INNER), jnp.float32)
    half = [jax.ShapeDtypeStruct(shape, jnp.bfloat16) for shape in ((tokens, width), (tokens, INNER))]
    return pl.pallas_call(
        second_kernel,
        out_shape=half + [state] * 3,
        in_specs=[IN_VMEM] * 5,
        out_specs=[IN_VMEM] * 5,
        scratch_shapes=[
            pltpu.VMEM(b.shape, jnp.bfloat16),
            pltpu.VMEM((tokens, 2 * INNER), jnp.bfloat16),
        ],
        compiler_params=pltpu.CompilerParams(vmem_limit_bytes=LIMIT),
        name="second_part",
    )(a, b, qkv, mod, w)


def uses(key_ref, count_ref, me, owner, blocks_here):
    used = jnp.bool_(False)
    for i in range(blocks_here):
        row = me * blocks_here + i
        for j in range(blocks_here, key_ref.shape[0]):
            used = used | ((key_ref[j, row] // blocks_here == owner) & (j < count_ref[row]))
    return used & (owner != me)


def project_block(block_ref, mod_ref, w_ref, normed, row, kv_ref):
    rows = slice(row, row + BLK)
    norm_rows(block_ref, mod_ref, normed, row)
    for c in range(0, 2 * INNER, 2 * PAIR):
        kv_ref[rows, c : c + 2 * PAIR] = project(normed[rows, :], w_ref, INNER + c, 2 * PAIR)


def arrived_kernel(count, exchanges, blocks_here, key_ref, count_ref, *rest):
    blocks, (mod_ref, w_ref, kv_ref, normed) = rest[: len(exchanges)], rest[len(exchanges) :]
    me = lax.axis_index("seq")
    partners = partners_here(me, count)
    for n, exchange in enumerate(exchanges):

        @pl.when(uses(key_ref, count_ref, me, partners[exchange], blocks_here))
        def _():
            project_block(blocks[n], mod_ref, w_ref, normed, n * BLK, kv_ref)


def arrived_part(count, exchanges, blocks_here, key_blocks, block_counts, blocks, mod, w):
    rows = len(exchanges) * BLK
    return pl.pallas_call(
        functools.partial(arrived_kernel, count, exchanges, blocks_here),
        out_shape=jax.ShapeDtypeStruct((rows, 2 * INNER), jnp.bfloat16),
        in_specs=[IN_SMEM] * 2 + [IN_VMEM] * (len(blocks) + 2),
        out_specs=IN_VMEM,
        scratch_shapes=[pltpu.VMEM((rows, w.shape[0]), jnp.bfloat16)],
        compiler_params=pltpu.CompilerParams(vmem_limit_bytes=LIMIT),
        name="arrived_part",
    )(key_blocks, block_counts, *blocks, mod, w)


def last_kernel(count, early, late, asked, pieces, key_ref, count_ref, *rest):
    early_ref, *rest = rest
    blocks, rest = rest[: len(late)], rest[len(late) :]
    q_ref, peak_ref, total_ref, acc_ref, x_ref, mod_ref, w_ref, wo_ref, *rest = rest
    if pieces == 1:
        y_out, normed, kv, attended, y_ref, sems = rest
        ys, sends, copies = [y_ref], [], []
    else:
        ys, sends, (normed, kv, attended) = rest[:pieces], rest[pieces:-3], rest[-3:]
    me = lax.axis_index("seq")
    tokens = x_ref.shape[0]
    blocks_here = tokens // BLK
    remote = key_ref.shape[0] - blocks_here
    partners = partners_here(me, count)
    slots = early + late
    for n, exchange in enumerate(slots):

        @pl.when(uses(key_ref, count_ref, me, partners[exchange], blocks_here))
        def _():
            if n < len(early):
                kv[n * BLK : (n + 1) * BLK, :] = early_ref[n * BLK : (n + 1) * BLK, :]
            else:
                project_block(blocks[n - len(early)], mod_ref, w_ref, normed, n * BLK, kv)

    starts, bias = [], []
    for i in range(blocks_here):
        row = me * blocks_here + i
        starts.append([])
        bias.append([])
        for j in range(remote):
            live = blocks_here + j < count_ref[row]
            bias[i].append(jnp.where(live, 0.0, MASKED))
            owner = key_ref[blocks_here + j, row] // blocks_here
            owner = jnp.where(live, owner, key_ref[blocks_here, row] // blocks_here)
            start = jnp.int32(0)
            for n, exchange in enumerate(slots):
                start = jnp.where(owner == partners[exchange], n * BLK, start)
            starts[i].append(pl.multiple_of(start, BLK))

    def listed(i, cols):
        return jnp.concatenate([kv[pl.ds(start, BLK), cols] for start in starts[i]], axis=0)

    def attend(i, at):
        here = slice(at, at + HD)
        rows = slice(i * BLK, (i + 1) * BLK)
        s = scores_of(q_ref[rows, here], listed(i, here))
        s = [s[:, j * BLK : (j + 1) * BLK] + bias[i][j] for j in range(remote)]
        old_peak = peak_ref[rows, here]
        peak = old_peak
        for part in s:
            peak = jnp.maximum(peak, jnp.max(part, axis=-1, keepdims=True))
        p = jnp.concatenate([jnp.exp2((part - peak) * TO_EXP2).astype(jnp.bfloat16) for part in s], axis=1)
        v = with_ones(listed(i, slice(INNER + at, INNER + at + HD)))
        both = jnp.dot(p, v, preferred_element_type=jnp.float32)
        keep = jnp.exp2((old_peak - peak) * TO_EXP2)
        total = total_ref[rows, here] * keep + both[:, HD:]
        acc = acc_ref[rows, here] * keep + both[:, :HD]
        attended[rows, here] = (acc / total).astype(jnp.bfloat16)

    def write(i, c):
        cols = slice(c, c + 2 * PAIR)
        rows = slice(i * BLK, (i + 1) * BLK)
        out = jnp.dot(attended[rows, :], wo_ref[:, cols], preferred_element_type=jnp.float32)
        y = (x_ref[rows, cols].astype(jnp.float32) + mod_ref[2, :, cols] * out).astype(jnp.bfloat16)
        each = tokens // pieces
        at = i * BLK % each
        ys[i * BLK // each][at : at + BLK, cols] = y
        if pieces == 1:
            copies.append(pltpu.make_async_copy(ys[0].at[rows, cols], y_out.at[rows, cols], sems.at[len(copies)]))
            copies[-1].start()

    waiting = []
    for i in range(blocks_here):
        for h in range(HEADS):
            attend(i, h * HD)
            if waiting and h % 4 == 3:
                write(*waiting.pop(0))
        waiting += [(i, c) for c in range(0, wo_ref.shape[1], 2 * PAIR)]
    for item in waiting:
        write(*item)
    send_asked(count, asked, key_ref, ys, sends)
    if pieces == 1:
        for copy in copies:
            copy.wait()


def last_part(count, early, late, asked, pieces, key_blocks, block_counts, early_kv, blocks, q, state, x, mod, w, wo):
    part = jax.ShapeDtypeStruct((BLK, x.shape[1]), x.dtype)
    piece = jax.ShapeDtypeStruct((x.shape[0] // pieces, x.shape[1]), x.dtype)
    slots = len(early) + len(late)
    written = []
    if pieces == 1:
        written = [pltpu.VMEM(x.shape, x.dtype), pltpu.SemaphoreType.DMA((wo.shape[1] // (2 * PAIR) * (x.shape[0] // BLK),))]
    return pl.pallas_call(
        functools.partial(last_kernel, count, early, late, asked, pieces),
        out_shape=[piece] * pieces + [part] * len(asked),
        in_specs=[IN_SMEM] * 2 + [IN_VMEM] * (9 + len(late)),
        out_specs=[IN_HBM] if pieces == 1 else [IN_VMEM] * (pieces + len(asked)),
        scratch_shapes=[
            pltpu.VMEM((slots * BLK, w.shape[0]), jnp.bfloat16),
            pltpu.VMEM((slots * BLK, 2 * INNER), jnp.bfloat16),
            pltpu.VMEM((x.shape[0], INNER), jnp.bfloat16),
        ]
        + written,
        compiler_params=pltpu.CompilerParams(vmem_limit_bytes=LIMIT),
        name="last_part",
    )(key_blocks, block_counts, early_kv, *blocks, q, *state, x, mod, w, wo)


def on_device(activations, qkv_weight, out_weight, modulation, key_blocks, block_counts):
    count = lax.axis_size("seq")
    sections = lax.axis_size("section")
    x, w, wo = activations[0], qkv_weight[0], out_weight[0]
    mod = modulation.reshape(modulation.shape[1], 1, modulation.shape[2])
    key_blocks = key_blocks.T
    lists_of = (key_blocks, block_counts)
    here = [(s, s) for s in range(sections)]
    onward = [(s, (s + 1) % sections) for s in range(sections)]

    def exchange(send, i, hops):
        pairs = [(s * count + a, t * count + b) for s, t in hops for a, b in pairs_of(i, count)]
        return lax.ppermute(send, ("section", "seq"), pairs)

    order = FIRST_EARLY + FIRST_LATE
    blocks_here = x.shape[0] // BLK
    got = {i: exchange(send, i, here) for i, send in zip(order, pick_blocks([x], key_blocks, count, order))}
    q, *state, w = first_part(x, mod, w)
    early = arrived_part(count, FIRST_EARLY, blocks_here, *lists_of, [got[i] for i in FIRST_EARLY], mod, w)
    blocks = [got[i] for i in FIRST_LATE]
    made = last_part(
        count, FIRST_EARLY, FIRST_LATE, SWAPPED, PIECES, *lists_of, early, blocks, q, state, x, mod, w, wo
    )
    pieces, sends = made[:PIECES], made[PIECES:]

    pieces = [lax.ppermute(piece, "section", onward) for piece in pieces]
    swapped = [exchange(send, i, here) for i, send in zip(SWAPPED, sends)]
    got = {i: lax.ppermute(block, "section", onward) for i, block in zip(SWAPPED, swapped)}
    qkv = half_part(pieces[0], mod, w)
    pieces[1], qkv = lax.optimization_barrier((pieces[1], qkv))
    relayed = tuple(i for i in order if i not in SWAPPED)
    params = pltpu.CompilerParams(vmem_limit_bytes=LIMIT)
    sends = pick_blocks(pieces, key_blocks, count, relayed, params)
    got.update({i: exchange(send, i, here) for i, send in zip(relayed, sends)})
    x, q, *state = second_part(*pieces, qkv, mod, w)
    early = arrived_part(count, SECOND_EARLY, blocks_here, *lists_of, [got[i] for i in SECOND_EARLY], mod, w)
    blocks = [got[i] for i in SECOND_LATE]
    (out,) = last_part(
        count, SECOND_EARLY, SECOND_LATE, (), 1, *lists_of, early, blocks, q, state, x, mod, w, wo
    )
    return out[None]


def solution(mesh):
    return jax.shard_map(
        on_device,
        mesh=mesh,
        in_specs=(
            P("section", "seq", None),
            P("section", None, None),
            P("section", None, None),
            P("section", None, None),
            P(),
            P(),
        ),
        out_specs=P("section", "seq", None),
        check_vma=False,
    )
```
